32 devices in a mesh: groups: 2 (over x), seq: 16 (over z, y, core).
Axes of the slice: x: 2, y: 2, z: 4, core: 2. Of those that a mesh axis runs over, the one named last changes fastest.
Arguments:
- frames: bfloat16 [16384, 1024], P(('groups', 'seq')), parts along dimension 0, may hold values from -6 to 6
- context: bfloat16 [3072, 512], P(('groups', 'seq')), parts along dimension 0, may hold values from -6 to 6
- noise_level: int32 [128], P(('groups', 'seq')), parts along dimension 0, may hold values from 0 to 7
- alignment: int32 [128, 2], P(('groups', 'seq')), parts along dimension 0, may hold values from 0 to 31, as said below
- counts: int32 [128], P(('groups', 'seq')), parts along dimension 0, may hold values from 1 to 2
- band_width: int32 [16], replicated, may hold values from 0 to 2, as said below
- mod_table: float32 [8, 2048], replicated, may hold values from -3 to 3
- qkv_weight: bfloat16 [1024, 3072], replicated, may hold values from -0.1875 to 0.1875
- out_weight: bfloat16 [1024, 1024], replicated, may hold values from -0.1875 to 0.1875
- cross_query_weight: bfloat16 [1024, 512], replicated, may hold values from -0.1875 to 0.1875
- cross_kv_weight: bfloat16 [512, 1024], replicated, may hold values from -0.25 to 0.25
- cross_out_weight: bfloat16 [512, 1024], replicated, may hold values from -0.25 to 0.25
- banded_attender_factor: float32 [16], replicated, may hold values from 0.5 to 80
- cross_temp: float32 [8], replicated, may hold values from 0.5 to 80
Outputs:
- update: bfloat16 [16384, 1024], P(('groups', 'seq')), parts along dimension 0
The draws below stay inside these ranges and needn't reach their ends.
There are 2 independent parts, one for each index of `groups`. The reference program is written for one: setup_inputs(seed, part) draws one part's arguments, and reference() takes and returns one part's arrays. A program takes and returns all parts, laid end to end along the dimension named above; an argument that names none is the same for every part. Nothing has to cross between parts.
Inputs may be any that keep to these rules, and one draw needn't show every extreme that they name: `alignment`: the entries of each list are distinct consecutive token blocks, all within 1 token blocks of (b * 2) // 4 for frame block b. Among the rows of one device, the list of the first frame block starts as low as that allows and the list of the last frame block ends as high as that allows and has all slots live, both within the excerpt's token blocks. `band_width`: some head has band width 2.
All inputs are finite; a program needn't handle non-finite values.
Results may differ from the reference program's by a relative error of at most 0.0045.
The reference program's roundings to bfloat16 on the way count: a program that leaves them out, or rounds other values in their place, can miss the bound.
Values may be sent and summed in bfloat16 or wider, within the bound.
No kernel may reach another device: no remote copies, remote signals or barrier semaphores. Data moves between devices by JAX's collectives and lax.ppermute only.
A program may use at most 192 MiB of HBM per device.

```python
import jax
import jax.numpy as jnp
from jax import lax

D = 1024
BANDED_ATTEND_CT = 16
MIXED_ATTEND_CNT = 8
HD = 64
CD = 512
LEVELS = 8
BLK = 128
WMAX = 2
TOKB = 48
RCH = 1
ALIST = 2
BPD = 4
QW = 1024
CQW = 512
TBD = 2
NBLK = 64
NTB = 32
FRAMES = 8192
TOKS = 1536


def alignment_pair(key):
    first_key, third_key = jax.random.split(jax.random.fold_in(key, 11), 2)
    blocks = jnp.arange(NBLK, dtype=jnp.int32)
    aligned = blocks * TBD // BPD
    lowest = jnp.maximum(-RCH, -aligned)
    upper_limit_value = jnp.minimum(RCH - ALIST + 1, NTB - ALIST - aligned)
    spread = jax.random.randint(first_key, (NBLK,), 0, 1000)
    offset = lowest + spread % (upper_limit_value - lowest + 1)
    first_of_device = blocks % BPD == 0
    last_of_device = blocks % BPD == BPD - 1
    offset = jnp.where(first_of_device, lowest, offset)
    offset = jnp.where(last_of_device, upper_limit_value, offset)
    lists = aligned[:, None] + offset[:, None] + jnp.arange(ALIST, dtype=jnp.int32)[None, :]
    live = jax.random.randint(third_key, (NBLK,), 1, ALIST + 1)
    live = jnp.where(last_of_device, ALIST, live)
    return (lists.astype(jnp.int32), live.astype(jnp.int32))


def draw_alignment(key, part):
    return alignment_pair(key)[0]


def draw_counts(key, part):
    return alignment_pair(key)[1]


def draw_band_width(key, part):
    first_key, second_key = jax.random.split(jax.random.fold_in(key, 23), 2)
    widths = jax.random.randint(first_key, (BANDED_ATTEND_CT,), 0, WMAX + 1)
    chosen = jax.random.randint(second_key, (), 0, BANDED_ATTEND_CT)
    return jnp.where(jnp.arange(BANDED_ATTEND_CT) == chosen, WMAX, widths).astype(jnp.int32)


def normalizer_heat_factors(key, attender_count):
    lowest, upper_limit_value = (0.5, 4.0)
    spread = jax.random.uniform(key, (attender_count,), jnp.float32, jnp.log(lowest), jnp.log(upper_limit_value))
    return jnp.exp(spread)


def draw_banded_attender_factor(key, part):
    return normalizer_heat_factors(jax.random.fold_in(key, 31), BANDED_ATTEND_CT)


def draw_cross_temp(key, part):
    return normalizer_heat_factors(jax.random.fold_in(key, 37), MIXED_ATTEND_CNT)


def touch_ends(array, key, least, top_value):
    dims = array.shape
    place = [jax.random.randint(jax.random.fold_in(key, axis), (), 0, dims[axis]) for axis in range(len(dims))]
    array = array.at[tuple(place)].set(least)
    longest = dims.index(max(dims))
    place[longest] = (place[longest] + 1) % dims[longest]
    return array.at[tuple(place)].set(top_value)


def block_scale(rng, extent, pieces, least, high):
    level = 1.0
    for axis_at, blocks in pieces:
        heights = jax.random.uniform(jax.random.fold_in(jax.random.fold_in(rng, 6), axis_at), (blocks,), jnp.float32, least / len(pieces), high / len(pieces))
        level = level * jnp.repeat(jnp.exp(heights), extent[axis_at] // blocks).reshape((-1,) + (1,) * (len(extent) - 1 - axis_at))
    return level


def noise(stream_key, dims, scale, most, pieces=(), kind=jnp.bfloat16):
    drawn = scale * jax.random.normal(stream_key, dims, jnp.float32)
    if pieces:
        drawn = drawn * block_scale(stream_key, dims, pieces, -0.22, 0.18)
    return jnp.clip(drawn, -most, most).astype(kind)


def setup_inputs(seed: int = 0, part: int = 0) -> dict:
    seeds = jax.random.split(jax.random.key(seed), 15)
    part_splits = jax.random.split(jax.random.fold_in(seeds[14], part), 15)
    return {
        "frames": noise(part_splits[0], (FRAMES, D), 1.0, 6.0, ((0, 16),)),
        "context": noise(part_splits[1], (TOKS, CD), 1.0, 6.0, ((0, 16),)),
        "noise_level": touch_ends(jax.random.randint(part_splits[2], (NBLK,), 0, LEVELS), jax.random.fold_in(part_splits[2], 1), 0, LEVELS - 1).astype(jnp.int32),
        "alignment": draw_alignment(jax.random.fold_in(jax.random.fold_in(seeds[14], part), 71), part),
        "counts": draw_counts(jax.random.fold_in(jax.random.fold_in(seeds[14], part), 71), part),
        "band_width": draw_band_width(jax.random.fold_in(seeds[14], 71), part),
        "mod_table": noise(seeds[6], (LEVELS, 2 * D), 0.5, 3.0, (), jnp.float32),
        "qkv_weight": noise(seeds[7], (D, 3 * QW), D ** -0.5, 0.1875),
        "out_weight": noise(seeds[8], (QW, D), QW ** -0.5, 0.1875),
        "cross_query_weight": noise(seeds[9], (D, CQW), D ** -0.5, 0.1875),
        "cross_kv_weight": noise(seeds[10], (CD, 2 * CQW), CD ** -0.5, 0.25),
        "cross_out_weight": noise(seeds[11], (CQW, D), CQW ** -0.5, 0.25),
        "banded_attender_factor": draw_banded_attender_factor(jax.random.fold_in(seeds[14], 71), part),
        "cross_temp": draw_cross_temp(jax.random.fold_in(seeds[14], 71), part),
    }


def head_norm(matrix, heads):
    count_rows = matrix.shape[0]
    parts = matrix.reshape(count_rows, heads, -1)
    parts = parts * lax.rsqrt(lax.optimization_barrier(jnp.mean(parts * parts, axis=-1, keepdims=True)) + 1e-06)
    return parts.reshape(count_rows, -1)

def masked_softmax(scores, allowed):
    scores = jnp.where(allowed, scores, -jnp.inf)
    peak = lax.optimization_barrier(jnp.max(scores, axis=-1, keepdims=True))
    powers = jnp.exp(scores - peak)
    return powers / lax.optimization_barrier(jnp.sum(powers, axis=-1, keepdims=True))

def reference(frames, context, noise_level, alignment, counts, band_width, mod_table, qkv_weight, out_weight, cross_query_weight, cross_kv_weight, cross_out_weight, banded_attender_factor, cross_temp):
    model_width = frames.shape[1]
    input_arrays = frames.astype(jnp.float32)
    normed = input_arrays * lax.rsqrt(lax.optimization_barrier(jnp.mean(input_arrays * input_arrays, axis=1, keepdims=True)) + 1e-06)
    modulation = mod_table[noise_level]
    hidden = (normed.reshape(NBLK, BLK, model_width) * (1.0 + modulation[:, None, :model_width]) + modulation[:, None, model_width:]).reshape(FRAMES, model_width).astype(jnp.bfloat16)
    projected = jnp.dot(hidden, qkv_weight, preferred_element_type=jnp.float32)
    queries = head_norm(projected[:, :QW], BANDED_ATTEND_CT).astype(jnp.bfloat16)
    keys_all = head_norm(projected[:, QW:2 * QW], BANDED_ATTEND_CT).astype(jnp.bfloat16)
    values_all = projected[:, 2 * QW:].astype(jnp.bfloat16)
    alignment_slack = WMAX * BLK
    lookup_vectors_padded = jnp.pad(keys_all, ((alignment_slack, alignment_slack), (0, 0)))
    values_pad = jnp.pad(values_all, ((alignment_slack, alignment_slack), (0, 0)))
    cross_queries = head_norm(jnp.dot(hidden, cross_query_weight, preferred_element_type=jnp.float32), MIXED_ATTEND_CNT).astype(jnp.bfloat16)
    cross_both = jnp.dot(context, cross_kv_weight, preferred_element_type=jnp.float32)
    cross_keys = head_norm(cross_both[:, :CQW], MIXED_ATTEND_CNT).astype(jnp.bfloat16)
    cross_values = cross_both[:, CQW:].astype(jnp.bfloat16)
    self_scale = banded_attender_factor * HD ** (-0.5)
    cross_scale = cross_temp * HD ** (-0.5)

    def one_block(block):
        first_row = block * BLK
        query_rows = lax.dynamic_slice_in_dim(queries, first_row, BLK, 0).astype(jnp.float32).reshape(BLK, BANDED_ATTEND_CT, HD)
        key_rows = lax.dynamic_slice_in_dim(lookup_vectors_padded, first_row, BLK + 2 * alignment_slack, 0).astype(jnp.float32).reshape(-1, BANDED_ATTEND_CT, HD)
        value_rows = lax.dynamic_slice_in_dim(values_pad, first_row, BLK + 2 * alignment_slack, 0).astype(jnp.float32).reshape(-1, BANDED_ATTEND_CT, HD)
        key_block = block - WMAX + jnp.arange(BLK + 2 * alignment_slack, dtype=jnp.int32) // BLK
        within_band_flag = (jnp.abs(block - key_block)[None, None, :] <= band_width[:, None, None]) & ((key_block >= 0) & (key_block < NBLK))[None, None, :]
        scores = jnp.einsum('ihd,jhd->hij', query_rows, key_rows) * self_scale[:, None, None]
        weights = lax.optimization_barrier(masked_softmax(scores, within_band_flag).astype(jnp.bfloat16)).astype(jnp.float32)
        self_out = jnp.einsum('hij,jhd->ihd', weights, value_rows).reshape(BLK, QW).astype(jnp.bfloat16)
        picked_keys = jnp.concatenate([lax.dynamic_slice_in_dim(cross_keys, (alignment[block, slot] * TOKB).astype(jnp.int32), TOKB, 0) for slot in range(ALIST)], 0)
        picked_values = jnp.concatenate([lax.dynamic_slice_in_dim(cross_values, (alignment[block, slot] * TOKB).astype(jnp.int32), TOKB, 0) for slot in range(ALIST)], 0)
        live = jnp.repeat(jnp.arange(ALIST, dtype=jnp.int32) < counts[block], TOKB)
        cross_rows = lax.dynamic_slice_in_dim(cross_queries, first_row, BLK, 0).astype(jnp.float32).reshape(BLK, MIXED_ATTEND_CNT, HD)
        cross_scores = jnp.einsum('ihd,jhd->hij', cross_rows, picked_keys.astype(jnp.float32).reshape(-1, MIXED_ATTEND_CNT, HD)) * cross_scale[:, None, None]
        cross_weights = lax.optimization_barrier(masked_softmax(cross_scores, live[None, None, :]).astype(jnp.bfloat16)).astype(jnp.float32)
        cross_out = jnp.einsum('hij,jhd->ihd', cross_weights, picked_values.astype(jnp.float32).reshape(-1, MIXED_ATTEND_CNT, HD)).reshape(BLK, CQW).astype(jnp.bfloat16)
        return (self_out, cross_out)
    self_all, cross_all = lax.map(one_block, jnp.arange(NBLK, dtype=jnp.int32))
    self_all = self_all.reshape(FRAMES, QW)
    cross_all = cross_all.reshape(FRAMES, CQW)
    total = jnp.dot(self_all, out_weight, preferred_element_type=jnp.float32) + jnp.dot(cross_all, cross_out_weight, preferred_element_type=jnp.float32)
    return total.astype(jnp.bfloat16)
```

```python
import functools

import jax
import jax.numpy as jnp
from jax import lax
from jax.experimental import pallas as pl
from jax.experimental.pallas import tpu as pltpu
from jax.sharding import PartitionSpec as P

BANDED_ATTEND_CT = 16
MIXED_ATTEND_CNT = 8
HD = 64
LEVELS = 8
BLK = 128
WMAX = 2
TOKB = 48
RCH = 1
ALIST = 2

LANES = 128
GROUP = 4
GCOLS = GROUP * HD
LOG2E = 1.4426950408889634
OFF = -1e30
PLAIN_FACTOR = 8.0
F32 = jnp.float32
BF16 = jnp.bfloat16
TOK_PACK = 32


def dot(a, b):
    return jnp.dot(a, b, preferred_element_type=F32)


def dot_t(a, b):
    return lax.dot_general(a, b, (((1,), (1,)), ((), ())), preferred_element_type=F32)


def head_mean(width):
    row = lax.broadcasted_iota(jnp.int32, (width, width), 0) // HD
    col = lax.broadcasted_iota(jnp.int32, (width, width), 1) // HD
    return jnp.where(row == col, 1.0 / HD, 0.0).astype(BF16)


def head_norm(x, mean):
    square = x * x
    high = square.astype(BF16)
    low = (square - high.astype(F32)).astype(BF16)
    ms = dot(high, mean) + dot(low, mean)
    return (x * lax.rsqrt(ms + 1e-06)).astype(BF16)


def low_half(rows):
    return lax.broadcasted_iota(jnp.int32, (rows, LANES), 1) < HD


def stack_pair(q):
    low = low_half(q.shape[0])
    zero = jnp.zeros_like(q)
    return jnp.concatenate([jnp.where(low, q, zero), jnp.where(low, zero, q)], 0)


def pair_attend(q, k, vext, scales, tile_bias, shifted):
    rows = q.shape[0]
    scores = dot_t(stack_pair(q), k)
    parts, shifts = [], []
    for head in range(2):
        mine = scores[head * rows : (head + 1) * rows]
        biases = tile_bias[head]
        width = k.shape[0] // len(biases)
        tiles = [
            mine[:, t * width : (t + 1) * width] * scales[head] + biases[t]
            for t in range(len(biases))
        ]
        if shifted:
            peak = tiles[0]
            for tile in tiles[1:]:
                peak = jnp.maximum(peak, tile)
            peak = jnp.max(peak, axis=1, keepdims=True)
            shifts.append(peak)
            tiles = [tile - peak for tile in tiles]
        tiles = [jnp.exp2(tile).astype(BF16) for tile in tiles]
        parts.append(tiles[0] if len(tiles) == 1 else jnp.concatenate(tiles, 1))
    got = dot(jnp.concatenate(parts, 0), vext)
    low = low_half(rows)
    total = jnp.where(low, got[:rows, :LANES], got[rows:, :LANES])
    weight = jnp.where(low, got[:rows, LANES:], got[rows:, LANES:])
    return total, weight, shifts


def band_bias(width, distance):
    return 0.0 if distance == 0 else jnp.where(width >= distance, 0.0, OFF).astype(F32)


def plain(factors, first, count):
    flag = factors[first] <= PLAIN_FACTOR
    for i in range(1, count):
        flag = flag & (factors[first + i] <= PLAIN_FACTOR)
    return flag


def token_bias(align, counts, block, first_token_block, window):
    place = lax.broadcasted_iota(jnp.int32, (1, window), 1) // TOKB + first_token_block
    allowed = place == align[block, 0]
    for slot in range(1, ALIST):
        live = jnp.where(slot < counts[block], align[block, slot], -RCH - 1)
        allowed = allowed | (place == live)
    return jnp.where(allowed, 0.0, OFF).astype(F32)


def local_block(f, odd, blocks):
    return jnp.where(odd, f, blocks - 1 - f)


def hidden_kernel(level, frames, table, context, hidden, near, far):
    odd = lax.rem(lax.axis_index("seq"), 2) == 1
    rows, width = frames.shape
    blocks = rows // BLK
    for b in range(blocks):
        at = pl.ds(b * BLK, BLK)
        x = frames[at, :].astype(F32)
        x = x * lax.rsqrt(jnp.mean(x * x, axis=1, keepdims=True) + 1e-06)
        row = table[pl.ds(level[b], 1), :]
        hidden[at, :] = (x * (1.0 + row[:, :width]) + row[:, width:]).astype(BF16)
    halo = WMAX * BLK
    tokens = context.shape[0]
    cwidth = context.shape[1]
    for pack, high in ((near, jnp.logical_not(odd)), (far, odd)):
        start = pl.multiple_of(jnp.where(high, rows - halo, 0), BLK)
        pack[:halo, :] = hidden[pl.ds(start, halo), :]
        start = pl.multiple_of(jnp.where(high, tokens - RCH * TOKB, 0), 16)
        tok = context[pl.ds(start, RCH * TOKB), :]
        pack[halo:, :cwidth] = tok[:TOK_PACK]
        pack[halo : halo + 16, cwidth:] = tok[TOK_PACK:]
        pack[halo + 16 :, cwidth:] = jnp.zeros((TOK_PACK - 16, cwidth), BF16)


def unpack_tokens(pack, halo, cwidth):
    return jnp.concatenate(
        [pack[halo : halo + TOK_PACK, :cwidth], pack[halo : halo + 16, cwidth:]], 0
    )


def main_kernel(
    band,
    factor,
    temp,
    align,
    counts,
    hidden,
    near,
    context,
    wq,
    wk,
    wv,
    wcq,
    wck,
    wcv,
    wo,
    wco,
    out,
    acc_out,
    sum_out,
    peak_out,
    q_out,
    cq_out,
    tok_out,
    window,
    pack,
    tokens,
    keys,
    vext,
    total,
    ready,
    sems,
):
    g = pl.program_id(0)
    device = lax.axis_index("seq")
    odd = lax.rem(device, 2) == 1
    rows = hidden.shape[0]
    blocks = rows // BLK
    halo = WMAX * BLK
    done = blocks - WMAX
    cwidth = context.shape[1]
    own = pl.multiple_of(jnp.where(odd, halo, 0), BLK)
    other = pl.multiple_of(jnp.where(odd, 0, rows), BLK)

    @pl.when(g == 0)
    def _():
        a = pltpu.make_async_copy(hidden, window.at[pl.ds(own, rows)], sems.at[0])
        b = pltpu.make_async_copy(
            near.at[pl.ds(0, halo)], window.at[pl.ds(other, halo)], sems.at[1]
        )
        c = pltpu.make_async_copy(near.at[pl.ds(halo, TOK_PACK)], pack, sems.at[2])
        a.start()
        b.start()
        c.start()
        vext[:, :, LANES:] = jnp.ones((2, window.shape[0], LANES), BF16)
        total[...] = jnp.zeros_like(total)
        tokens[...] = jnp.zeros_like(tokens)
        tokens[RCH * TOKB : RCH * TOKB + context.shape[0], :] = context[...]
        c.wait()
        start = jnp.where(odd, 0, RCH * TOKB + context.shape[0])
        tokens[pl.ds(pl.multiple_of(start, 16), RCH * TOKB), :] = unpack_tokens(pack, 0, cwidth)
        a.wait()
        b.wait()

    mean = head_mean(GCOLS)
    q = head_norm(dot(window[pl.ds(own, rows), :], wq[...]), mean)
    ready[0] = q
    keys[...] = head_norm(dot(window[...], wk[...]), mean)
    values = dot(window[...], wv[...]).astype(BF16)
    for pair in range(2):
        vext[pair, :, :LANES] = values[:, pair * LANES : (pair + 1) * LANES]
    cq = head_norm(dot(window[pl.ds(own, rows), :], wcq[...]), mean[:LANES, :LANES])
    ready[1, :, :LANES] = cq
    ck = head_norm(dot(tokens[...], wck[...]), mean[:LANES, :LANES])
    cv = dot(tokens[...], wcv[...]).astype(BF16)
    cvext = jnp.concatenate([cv, jnp.ones_like(cv)], 1)
    tok_out[...] = tokens[...]
    for f in range(done, blocks):
        start = pl.multiple_of(local_block(f, odd, blocks) * BLK, BLK)
        at = pl.ds((f - done) * BLK, BLK)
        q_out[at, :] = ready[0, pl.ds(start, BLK), :]
        cq_out[at, :] = ready[1, pl.ds(start, BLK), :LANES]

    def self_part(shifted):
        if shifted:

            @pl.when(g == 0)
            def _():
                peak_out[...] = jnp.zeros_like(peak_out)

        outs = [[], []]
        for pair in range(2):
            heads = [g * GROUP + 2 * pair + i for i in range(2)]
            scales = [factor[h] * (HD**-0.5 * LOG2E) for h in heads]
            lanes = slice(pair * LANES, (pair + 1) * LANES)
            for f in range(blocks):
                inner = min(WMAX, blocks - 1 - f)
                count = WMAX + 1 + inner
                start = pl.multiple_of(local_block(f, odd, blocks) * BLK, BLK)
                first = pl.multiple_of(jnp.where(odd, f, blocks - 1 - f - inner) * BLK, BLK)
                at = pl.ds(first, count * BLK)
                bias = [
                    [
                        jnp.where(
                            odd,
                            band_bias(band[h], abs(t - WMAX)),
                            band_bias(band[h], abs(t - inner)),
                        )
                        for t in range(count)
                    ]
                    for h in heads
                ]
                part, weight, shifts = pair_attend(
                    ready[0, pl.ds(start, BLK), lanes],
                    keys[at, lanes],
                    vext[pair, at, :],
                    scales,
                    bias,
                    shifted,
                )
                if f < done:
                    outs[f].append((part / weight).astype(BF16))
                else:
                    to = slice((f - done) * BLK, (f - done + 1) * BLK)
                    acc_out[to, lanes] = part
                    sum_out[to, lanes] = weight
                    if shifted:
                        lane = lax.broadcasted_iota(jnp.int32, (BLK, LANES), 1)
                        peaks = peak_out[to, :]
                        for h, shift in zip(heads, shifts):
                            peaks = jnp.where(lane == h, shift, peaks)
                        peak_out[to, :] = peaks
        mine = jnp.concatenate([jnp.concatenate(o, 1) for o in outs], 0)
        total[...] += dot(mine, wo[...])

    def cross_part(shifted):
        heads = [2 * g, 2 * g + 1]
        scales = [temp[h] * (HD**-0.5 * LOG2E) for h in heads]
        first = device * (context.shape[0] // TOKB) - RCH
        outs = []
        for f in range(done):
            block = local_block(f, odd, blocks)
            start = pl.multiple_of(block * BLK, BLK)
            bias = token_bias(align, counts, block, first, tokens.shape[0])
            part, weight, _ = pair_attend(
                ready[1, pl.ds(start, BLK), :LANES],
                ck,
                cvext,
                scales,
                [[bias], [bias]],
                shifted,
            )
            outs.append((part / weight).astype(BF16))
        total[...] += dot(jnp.concatenate(outs, 0), wco[...])

    easy = plain(factor, g * GROUP, GROUP)
    pl.when(easy)(lambda: self_part(False))
    pl.when(jnp.logical_not(easy))(lambda: self_part(True))
    easy = plain(temp, 2 * g, 2)
    pl.when(easy)(lambda: cross_part(False))
    pl.when(jnp.logical_not(easy))(lambda: cross_part(True))

    @pl.when(g == pl.num_programs(0) - 1)
    def _():
        finish(total, out, window, sems, 0, done, odd, blocks)


def finish(total, out, stage, sems, first, count, odd, blocks):
    copies = []
    for i in range(count):
        at = pl.ds(i * BLK, BLK)
        stage[at, :] = total[at, :].astype(BF16)
        to = pl.multiple_of(local_block(first + i, odd, blocks) * BLK, BLK)
        copies.append(
            pltpu.make_async_copy(stage.at[at], out.at[pl.ds(to, BLK)], sems.at[i])
        )
        copies[-1].start()
    for copy in copies:
        copy.wait()


def tail_kernel(
    blocks,
    band,
    factor,
    temp,
    align,
    counts,
    pack,
    wk,
    wv,
    wck,
    wcv,
    wo,
    wco,
    acc_in,
    sum_in,
    peak_in,
    q_in,
    cq_in,
    tok_in,
    partial_out,
    out,
    tokens,
    keys,
    vext,
    total,
    stage,
    sems,
):
    g = pl.program_id(0)
    device = lax.axis_index("seq")
    odd = lax.rem(device, 2) == 1
    last = lax.axis_size("seq") - 1
    exists = jnp.where(odd, device < last, device > 0)
    halo = WMAX * BLK
    done = blocks - WMAX
    cwidth = tok_in.shape[1]
    window = tok_in.shape[0]

    @pl.when(g == 0)
    def _():
        vext[:, :, LANES:] = jnp.ones((2, halo, LANES), BF16)
        total[...] = jnp.zeros_like(total)
        tokens[...] = tok_in[...]
        start = jnp.where(odd, window - RCH * TOKB, 0)
        tokens[pl.ds(pl.multiple_of(start, 16), RCH * TOKB), :] = unpack_tokens(
            pack, halo, cwidth
        )

    mean = head_mean(GCOLS)
    rows = pack[:halo, :]
    keys[...] = head_norm(dot(rows, wk[...]), mean)
    values = dot(rows, wv[...]).astype(BF16)
    for pair in range(2):
        vext[pair, :, :LANES] = values[:, pair * LANES : (pair + 1) * LANES]
    ck = head_norm(dot(tokens[...], wck[...]), mean[:LANES, :LANES])
    cv = dot(tokens[...], wcv[...]).astype(BF16)
    cvext = jnp.concatenate([cv, jnp.ones_like(cv)], 1)

    def self_part(shifted):
        outs = [[] for _ in range(WMAX)]
        low = low_half(BLK)
        for pair in range(2):
            heads = [g * GROUP + 2 * pair + i for i in range(2)]
            scales = [factor[h] * (HD**-0.5 * LOG2E) for h in heads]
            widths = [jnp.where(exists, band[h], 0) for h in heads]
            lanes = slice(pair * LANES, (pair + 1) * LANES)
            for f in range(done, blocks):
                inner = blocks - 1 - f
                count = WMAX - inner
                first = pl.multiple_of(jnp.where(odd, 0, halo - count * BLK), BLK)
                at = pl.ds(first, count * BLK)
                bias = [
                    [
                        jnp.where(
                            odd,
                            band_bias(w, inner + 1 + t),
                            band_bias(w, inner + count - t),
                        )
                        for t in range(count)
                    ]
                    for w in widths
                ]
                to = slice((f - done) * BLK, (f - done + 1) * BLK)
                part, weight, shifts = pair_attend(
                    q_in[to, lanes], keys[at, lanes], vext[pair, at, :], scales, bias, shifted
                )
                had, had_weight = acc_in[to, lanes], sum_in[to, lanes]
                if shifted:
                    lane = lax.broadcasted_iota(jnp.int32, (BLK, LANES), 1)
                    olds = [
                        jnp.sum(
                            jnp.where(lane == h, peak_in[to, :], 0.0), axis=1, keepdims=True
                        )
                        for h in heads
                    ]
                    news = [jnp.maximum(a, b) for a, b in zip(olds, shifts)]
                    keep = [jnp.exp2(a - n) for a, n in zip(olds, news)]
                    add = [jnp.exp2(b - n) for b, n in zip(shifts, news)]
                    keep = jnp.where(low, keep[0], keep[1])
                    add = jnp.where(low, add[0], add[1])
                    had, had_weight = had * keep, had_weight * keep
                    part, weight = part * add, weight * add
                outs[f - done].append(((had + part) / (had_weight + weight)).astype(BF16))
        mine = jnp.concatenate([jnp.concatenate(o, 1) for o in outs], 0)
        total[...] += dot(mine, wo[...])

    def cross_part(shifted):
        heads = [2 * g, 2 * g + 1]
        scales = [temp[h] * (HD**-0.5 * LOG2E) for h in heads]
        first = device * (window // TOKB - 2 * RCH) - RCH
        outs = []
        for f in range(done, blocks):
            block = local_block(f, odd, blocks)
            bias = token_bias(align, counts, block, first, window)
            to = slice((f - done) * BLK, (f - done + 1) * BLK)
            part, weight, _ = pair_attend(
                cq_in[to, :], ck, cvext, scales, [[bias], [bias]], shifted
            )
            outs.append((part / weight).astype(BF16))
        total[...] += dot(jnp.concatenate(outs, 0), wco[...])

    easy = plain(factor, g * GROUP, GROUP)
    pl.when(easy)(lambda: self_part(False))
    pl.when(jnp.logical_not(easy))(lambda: self_part(True))
    easy = plain(temp, 2 * g, 2)
    pl.when(easy)(lambda: cross_part(False))
    pl.when(jnp.logical_not(easy))(lambda: cross_part(True))

    @pl.when(g == pl.num_programs(0) - 1)
    def _():
        finish(total, out, stage, sems, done, WMAX, odd, blocks)


def shards(
    frames,
    context,
    noise_level,
    alignment,
    counts,
    band_width,
    mod_table,
    qkv_weight,
    out_weight,
    cross_query_weight,
    cross_kv_weight,
    cross_out_weight,
    banded_attender_factor,
    cross_temp,
):
    rows, width = frames.shape
    blocks = rows // BLK
    halo = WMAX * BLK
    done = blocks - WMAX
    tokens, cwidth = context.shape
    query_width = qkv_weight.shape[1] // 3
    cross_width = cross_query_weight.shape[1]
    steps = query_width // GCOLS
    ccols = cross_width // steps
    token_window = tokens + 2 * RCH * TOKB
    devices = lax.axis_size("seq")
    smem = pl.BlockSpec(memory_space=pltpu.SMEM)
    vmem = pl.BlockSpec(memory_space=pltpu.VMEM)
    anywhere = pl.BlockSpec(memory_space=pl.ANY)
    pack_rows = halo + TOK_PACK

    hidden, near, far = pl.pallas_call(
        hidden_kernel,
        out_shape=[
            jax.ShapeDtypeStruct((rows, width), BF16),
            jax.ShapeDtypeStruct((pack_rows, width), BF16),
            jax.ShapeDtypeStruct((pack_rows, width), BF16),
        ],
        in_specs=[smem, vmem, vmem, vmem],
        out_specs=[vmem, vmem, vmem],
        name="hidden_and_packs",
    )(noise_level, frames, mod_table, context)

    same_chip = [(i, i ^ 1) for i in range(devices) if i ^ 1 < devices]
    across = [(i, i + 1) for i in range(1, devices - 1, 2)]
    across += [(b, a) for a, b in across]
    far_got = lax.ppermute(far, "seq", across)
    near_got = lax.ppermute(near, "seq", same_chip)

    def column(block_rows, cols, offset):
        return pl.BlockSpec((block_rows, cols), lambda g: (0, g + offset))

    def row(block_rows, cols):
        return pl.BlockSpec((block_rows, cols), lambda g: (g, 0))

    def whole(*shape):
        return pl.BlockSpec(shape, lambda g: (0,) * len(shape))

    open_rows = WMAX * BLK
    update, acc, weight, peaks, q_open, cq_open, window_tokens = pl.pallas_call(
        main_kernel,
        grid=(steps,),
        out_shape=[
            jax.ShapeDtypeStruct((rows, width), BF16),
            jax.ShapeDtypeStruct((open_rows, query_width), F32),
            jax.ShapeDtypeStruct((open_rows, query_width), F32),
            jax.ShapeDtypeStruct((open_rows, LANES), F32),
            jax.ShapeDtypeStruct((open_rows, query_width), BF16),
            jax.ShapeDtypeStruct((open_rows, cross_width), BF16),
            jax.ShapeDtypeStruct((token_window, cwidth), BF16),
        ],
        in_specs=[smem] * 5
        + [
            anywhere,
            anywhere,
            whole(tokens, cwidth),
            column(width, GCOLS, 0),
            column(width, GCOLS, steps),
            column(width, GCOLS, 2 * steps),
            column(width, ccols, 0),
            column(cwidth, ccols, 0),
            column(cwidth, ccols, steps),
            row(GCOLS, width),
            row(ccols, width),
        ],
        out_specs=[
            anywhere,
            column(open_rows, GCOLS, 0),
            column(open_rows, GCOLS, 0),
            whole(open_rows, LANES),
            column(open_rows, GCOLS, 0),
            column(open_rows, ccols, 0),
            whole(token_window, cwidth),
        ],
        scratch_shapes=[
            pltpu.VMEM((rows + halo, width), BF16),
            pltpu.VMEM((TOK_PACK, width), BF16),
            pltpu.VMEM((token_window, cwidth), BF16),
            pltpu.VMEM((rows + halo, GCOLS), BF16),
            pltpu.VMEM((2, rows + halo, 2 * LANES), BF16),
            pltpu.VMEM((done * BLK, width), F32),
            pltpu.VMEM((2, rows, GCOLS), BF16),
            pltpu.SemaphoreType.DMA((max(3, done),)),
        ],
        compiler_params=pltpu.CompilerParams(vmem_limit_bytes=48 * 2**20),
        cost_estimate=pl.CostEstimate(
            flops=12 * 10**9, bytes_accessed=20 * 10**6, transcendentals=5 * 10**6
        ),
        name="local_attention",
    )(
        band_width,
        banded_attender_factor,
        cross_temp,
        alignment,
        counts,
        hidden,
        near_got,
        context,
        qkv_weight,
        qkv_weight,
        qkv_weight,
        cross_query_weight,
        cross_kv_weight,
        cross_kv_weight,
        out_weight,
        cross_out_weight,
    )

    return pl.pallas_call(
        functools.partial(tail_kernel, blocks),
        grid=(steps,),
        out_shape=jax.ShapeDtypeStruct((rows, width), BF16),
        in_specs=[smem] * 5
        + [
            whole(pack_rows, width),
            column(width, GCOLS, steps),
            column(width, GCOLS, 2 * steps),
            column(cwidth, ccols, 0),
            column(cwidth, ccols, steps),
            row(GCOLS, width),
            row(ccols, width),
            column(open_rows, GCOLS, 0),
            column(open_rows, GCOLS, 0),
            whole(open_rows, LANES),
            column(open_rows, GCOLS, 0),
            column(open_rows, ccols, 0),
            whole(token_window, cwidth),
            anywhere,
        ],
        out_specs=anywhere,
        scratch_shapes=[
            pltpu.VMEM((token_window, cwidth), BF16),
            pltpu.VMEM((halo, GCOLS), BF16),
            pltpu.VMEM((2, halo, 2 * LANES), BF16),
            pltpu.VMEM((open_rows, width), F32),
            pltpu.VMEM((open_rows, width), BF16),
            pltpu.SemaphoreType.DMA((WMAX,)),
        ],
        input_output_aliases={18: 0},
        compiler_params=pltpu.CompilerParams(vmem_limit_bytes=48 * 2**20),
        cost_estimate=pl.CostEstimate(
            flops=5 * 10**9, bytes_accessed=12 * 10**6, transcendentals=10**6
        ),
        name="halo_attention",
    )(
        band_width,
        banded_attender_factor,
        cross_temp,
        alignment,
        counts,
        far_got,
        qkv_weight,
        qkv_weight,
        cross_kv_weight,
        cross_kv_weight,
        out_weight,
        cross_out_weight,
        acc,
        weight,
        peaks,
        q_open,
        cq_open,
        window_tokens,
        update,
    )


def solution(mesh):
    placed = (
        P(("groups", "seq"), None),
        P(("groups", "seq"), None),
        P(("groups", "seq")),
        P(("groups", "seq"), None),
        P(("groups", "seq")),
        P(),
        P(),
        P(),
        P(),
        P(),
        P(),
        P(),
        P(),
        P(),
    )
    return jax.shard_map(
        shards, mesh=mesh, in_specs=placed, out_specs=P(("groups", "seq"), None), check_vma=False
    )
```

```python
import jax
import jax.numpy as jnp
from jax import lax
from jax.experimental import pallas as pl
from jax.experimental.pallas import tpu as pltpu
from jax.sharding import PartitionSpec as P

BANDED_ATTEND_CT = 16
MIXED_ATTEND_CNT = 8
HD = 64
LEVELS = 8
BLK = 128
WMAX = 2
TOKB = 48
RCH = 1
ALIST = 2

LANES = 128
CHUNK = 512
TILE = 256
LOG2E = 1.4426950408889634
OFF = -1e30
PLAIN_FACTOR = 8.0
F32 = jnp.float32
BF16 = jnp.bfloat16
MAIN_VMEM = 32 * 2**20
TAIL_VMEM = 16 * 2**20
TOK_PACK = 32


def dot(a, b):
    return jnp.dot(a, b, preferred_element_type=F32)


def dot_t(a, b):
    return lax.dot_general(a, b, (((1,), (1,)), ((), ())), preferred_element_type=F32)


def low_half(rows):
    return lax.broadcasted_iota(jnp.int32, (rows, LANES), 1) < HD


def head_norm(x):
    low = low_half(x.shape[0])
    done = []
    for start in range(0, x.shape[1], LANES):
        pair = x[:, start : start + LANES]
        square = pair * pair
        first = jnp.sum(jnp.where(low, square, 0.0), axis=1, keepdims=True)
        second = jnp.sum(jnp.where(low, 0.0, square), axis=1, keepdims=True)
        mean = jnp.where(low, first, second) * (1.0 / HD)
        done.append((pair * lax.rsqrt(mean + 1e-06)).astype(BF16))
    return jnp.concatenate(done, 1)


def staggered(items, delay=1):
    begun = []
    for begin, end in items:
        begun.append((end, begin()))
        if len(begun) > delay:
            end, value = begun.pop(0)
            end(value)
    for end, value in begun:
        end(value)


def pair_scores(q, k):
    low = low_half(q.shape[0])
    zero = jnp.zeros_like(q)
    stacked = jnp.concatenate([jnp.where(low, q, zero), jnp.where(low, zero, q)], 0)
    return dot_t(stacked, k)


def pair_sums(scores, vext, scales, tile_bias, shifted):
    rows = scores.shape[0] // 2
    parts, shifts = [], []
    for head in range(2):
        mine = scores[head * rows : (head + 1) * rows]
        biases = tile_bias[head]
        width = mine.shape[1] // len(biases)
        tiles = []
        for t, bias in enumerate(biases):
            tile = mine[:, t * width : (t + 1) * width] * scales[head]
            tiles.append(tile if bias is None else tile + bias)
        if shifted:
            peak = tiles[0]
            for tile in tiles[1:]:
                peak = jnp.maximum(peak, tile)
            peak = jnp.max(peak, axis=1, keepdims=True)
            shifts.append(peak)
            tiles = [tile - peak for tile in tiles]
        tiles = [jnp.exp2(tile).astype(BF16) for tile in tiles]
        parts.append(tiles[0] if len(tiles) == 1 else jnp.concatenate(tiles, 1))
    got = dot(jnp.concatenate(parts, 0), vext)
    low = low_half(rows)
    total = jnp.where(low, got[:rows, :LANES], got[rows:, :LANES])
    weight = jnp.where(low, got[:rows, LANES:], got[rows:, LANES:])
    return total, weight, shifts


def band_bias(width, distance):
    return jnp.where(width >= distance, 0.0, OFF).astype(F32)


def plain(factor, temp):
    flag = factor[0] <= PLAIN_FACTOR
    for i in range(1, BANDED_ATTEND_CT):
        flag = flag & (factor[i] <= PLAIN_FACTOR)
    for i in range(MIXED_ATTEND_CNT):
        flag = flag & (temp[i] <= PLAIN_FACTOR)
    return flag


def token_bias(align, counts, block, first_token_block, window):
    place = lax.broadcasted_iota(jnp.int32, (1, window), 1) // TOKB + first_token_block
    allowed = place == align[0, block]
    for slot in range(1, ALIST):
        live = jnp.where(slot < counts[block], align[slot, block], -RCH - 1)
        allowed = allowed | (place == live)
    return jnp.where(allowed, 0.0, OFF).astype(F32)


def local_block(f, odd, blocks):
    return jnp.where(odd, f, blocks - 1 - f)


def in_hbm(*arrays):
    return [pltpu.with_memory_space_constraint(a, pltpu.HBM) for a in arrays]


def lanes_of(pair):
    if isinstance(pair, int):
        return slice(pair * LANES, (pair + 1) * LANES)
    return pl.ds(pl.multiple_of(pair * LANES, LANES), LANES)


def hidden_kernel(level, frames, table, context, hidden, near, far, stage, sems):
    odd = lax.rem(lax.axis_index("seq"), 2) == 1
    rows, width = frames.shape
    blocks = rows // BLK
    copies = []
    for b in range(blocks):
        at = pl.ds(b * BLK, BLK)
        copies.append(pltpu.make_async_copy(frames.at[at], stage.at[at], sems.at[b]))
        copies[-1].start()
    for b in range(blocks):
        at = pl.ds(b * BLK, BLK)
        row = table[pl.ds(level[b], 1), :]
        copies[b].wait()
        x = stage[at, :].astype(F32)
        x = x * lax.rsqrt(jnp.mean(x * x, axis=1, keepdims=True) + 1e-06)
        hidden[at, :] = (x * (1.0 + row[:, :width]) + row[:, width:]).astype(BF16)
    halo = WMAX * BLK
    tokens = context.shape[0]
    cwidth = context.shape[1]
    for pack, high in ((near, jnp.logical_not(odd)), (far, odd)):
        start = pl.multiple_of(jnp.where(high, rows - halo, 0), BLK)
        pack[:halo, :] = hidden[pl.ds(start, halo), :]
        start = pl.multiple_of(jnp.where(high, tokens - RCH * TOKB, 0), 16)
        tok = context[pl.ds(start, RCH * TOKB), :]
        pack[halo:, :cwidth] = tok[:TOK_PACK]
        pack[halo : halo + 16, cwidth:] = tok[TOK_PACK:]
        pack[halo + 16 :, cwidth:] = jnp.zeros((TOK_PACK - 16, cwidth), BF16)


def unpack_tokens(pack, halo, cwidth):
    return jnp.concatenate(
        [pack[halo : halo + TOK_PACK, :cwidth], pack[halo : halo + 16, cwidth:]], 0
    )


def token_pairs(tokens, wckv, ck, cvext):
    cwidth = ck.shape[1]
    x = tokens[...]
    ck[...] = head_norm(dot(x, wckv[:, :cwidth]))
    values = dot(x, wckv[:, cwidth:]).astype(BF16)
    for pair in range(cwidth // LANES):
        cvext[pair, :, :LANES] = values[:, lanes_of(pair)]


def store_values(vext, at, start, values):
    for i in range(values.shape[1] // LANES):
        vext[start // LANES + i, at, :LANES] = values[:, lanes_of(i)]


def scalar_copies(sources, targets, sems, first):
    copies = []
    for i, (source, target) in enumerate(zip(sources, targets)):
        copies.append(pltpu.make_async_copy(source, target, sems.at[first + i]))
        copies[-1].start()
    return copies


def finish(total, out, stage, sems, first, count, odd, blocks):
    copies = []
    for i in range(count):
        at = pl.ds(i * BLK, BLK)
        stage[at, :] = total[i * BLK : (i + 1) * BLK].astype(BF16)
        to = pl.multiple_of(local_block(first + i, odd, blocks) * BLK, BLK)
        copies.append(
            pltpu.make_async_copy(stage.at[at], out.at[pl.ds(to, BLK)], sems.at[i])
        )
        copies[-1].start()
    for copy in copies:
        copy.wait()


def main_kernel(
    band_in,
    factor_in,
    temp_in,
    align_in,
    counts_in,
    hidden,
    near,
    context,
    wqkv_in,
    wcq_in,
    wckv_in,
    wo_in,
    wco_in,
    out,
    acc_out,
    sum_out,
    peak_out,
    q,
    cq,
    band,
    factor,
    temp,
    align,
    counts,
    wqkv,
    wcq,
    wckv,
    wo,
    wco,
    tokens,
    keys,
    vext,
    ck,
    cvext,
    mine,
    cross_mine,
    stage,
    sems,
):
    device = lax.axis_index("seq")
    odd = lax.rem(device, 2) == 1
    rows = hidden.shape[0]
    blocks = rows // BLK
    halo = WMAX * BLK
    done = blocks - WMAX
    qwidth = q.shape[1]
    cwidth = context.shape[1]
    own = jnp.where(odd, halo, 0)
    other = jnp.where(odd, 0, rows)

    loads = []
    for start in range(0, 3 * qwidth, CHUNK):
        cols = pl.ds(start, CHUNK)
        loads.append((wqkv_in.at[:, cols], wqkv.at[:, cols]))
    loads += [(wcq_in, wcq), (wckv_in, wckv), (wo_in, wo), (wco_in, wco)]
    loads = [pltpu.make_async_copy(a, b, sems.at[i]) for i, (a, b) in enumerate(loads)]
    for load in loads[:2]:
        load.start()
    scalars = scalar_copies(
        (band_in, factor_in, temp_in, align_in, counts_in),
        (band, factor, temp, align, counts),
        sems,
        len(loads),
    )
    for load in loads[2:]:
        load.start()

    vext[:, :, LANES:] = jnp.ones((vext.shape[0], vext.shape[1], LANES), BF16)
    cvext[:, :, LANES:] = jnp.ones((cvext.shape[0], cvext.shape[1], LANES), BF16)
    tokens[...] = jnp.zeros_like(tokens)
    tokens[RCH * TOKB : RCH * TOKB + context.shape[0], :] = context[...]
    start = jnp.where(odd, 0, RCH * TOKB + context.shape[0])
    tokens[pl.ds(pl.multiple_of(start, 16), RCH * TOKB), :] = unpack_tokens(near, halo, cwidth)

    def project(source, first, to, start):
        def begin():
            return dot(source[first : first + TILE, :], wqkv[:, start : start + CHUNK])

        def end(x):
            at = pl.ds(pl.multiple_of(to + first, BLK), TILE)
            part, col = divmod(start, qwidth)
            if part == 0:
                q[first : first + TILE, col : col + CHUNK] = head_norm(x)
            elif part == 1:
                keys[at, col : col + CHUNK] = head_norm(x)
            else:
                store_values(vext, at, col, x.astype(BF16))

        return begin, end

    def project_cross(first):
        def begin():
            return dot(hidden[first : first + TILE, :], wcq[...])

        def end(x):
            cq[first : first + TILE, :] = head_norm(x)

        return begin, end

    items = []
    for i, start in enumerate(range(0, 3 * qwidth, CHUNK)):
        tiles = [project(hidden, first, own, start) for first in range(0, rows, TILE)]
        if start >= qwidth:
            tiles += [project(near, first, other, start) for first in range(0, halo, TILE)]
        begin, end = tiles[0]
        tiles[0] = (lambda i=i, begin=begin: (loads[i].wait(), begin())[1], end)
        items += tiles
    staggered(items)
    count = 3 * qwidth // CHUNK
    loads[count].wait()
    loads[count + 1].wait()
    staggered([project_cross(first) for first in range(0, rows, TILE)])
    token_pairs(tokens, wckv, ck, cvext)
    for copy in scalars:
        copy.wait()

    def self_item(pair, f, shifted):
        heads = [2 * pair, 2 * pair + 1]
        lanes = lanes_of(pair)
        inner = min(WMAX, blocks - 1 - f)
        count = WMAX + 1 + inner
        start = pl.multiple_of(local_block(f, odd, blocks) * BLK, BLK)
        first = pl.multiple_of(jnp.where(odd, f, blocks - 1 - f - inner) * BLK, BLK)
        at = pl.ds(first, count * BLK)

        def begin():
            return pair_scores(q[pl.ds(start, BLK), lanes], keys[at, lanes])

        def end(scores):
            bias = [[] for _ in heads]
            for mine_bias, h in zip(bias, heads):
                by_distance = [0.0] + [band_bias(band[h], d) for d in range(1, WMAX + 1)]
                for t in range(count):
                    one, two = abs(t - WMAX), abs(t - inner)
                    if one == two:
                        mine_bias.append(None if one == 0 else by_distance[one])
                    else:
                        mine_bias.append(jnp.where(odd, by_distance[one], by_distance[two]))
            scales = [factor[h] * (HD**-0.5 * LOG2E) for h in heads]
            part, weight, shifts = pair_sums(scores, vext[pair, at, :], scales, bias, shifted)
            if f < done:
                mine[f * BLK : (f + 1) * BLK, lanes] = (part / weight).astype(BF16)
                return
            to = slice((f - done) * BLK, (f - done + 1) * BLK)
            acc_out[to, lanes] = part
            sum_out[to, lanes] = weight
            if shifted:
                lane = lax.broadcasted_iota(jnp.int32, (BLK, LANES), 1)
                peaks = peak_out[to, :]
                for h, shift in zip(heads, shifts):
                    peaks = jnp.where(lane == h, shift, peaks)
                peak_out[to, :] = peaks

        return begin, end

    biases = [
        token_bias(
            align,
            counts,
            local_block(f, odd, blocks),
            device * (context.shape[0] // TOKB) - RCH,
            tokens.shape[0],
        )
        for f in range(done)
    ]

    def cross_item(pair, f, shifted):
        lanes = lanes_of(pair)
        start = pl.multiple_of(local_block(f, odd, blocks) * BLK, BLK)

        def begin():
            return pair_scores(cq[pl.ds(start, BLK), lanes], ck[:, lanes])

        def end(scores):
            scales = [temp[2 * pair + i] * (HD**-0.5 * LOG2E) for i in range(2)]
            part, weight, _ = pair_sums(
                scores, cvext[pair], scales, [[biases[f]]] * 2, shifted
            )
            cross_mine[f * BLK : (f + 1) * BLK, lanes] = (part / weight).astype(BF16)

        return begin, end

    pairs, cross_pairs = qwidth // LANES, cwidth // LANES
    easy = plain(factor, temp)

    @pl.when(easy)
    def _():
        items = [cross_item(p, f, False) for p in range(cross_pairs) for f in range(done)]
        items += [self_item(p, f, False) for p in range(pairs) for f in range(blocks)]
        staggered(items)

    @pl.when(jnp.logical_not(easy))
    def _():
        peak_out[...] = jnp.zeros_like(peak_out)

        @pl.loop(0, pairs)
        def _(p):
            staggered([self_item(p, f, True) for f in range(blocks)])

        @pl.loop(0, cross_pairs)
        def _(p):
            staggered([cross_item(p, f, True) for f in range(done)])

    for load in loads[count + 2 :]:
        load.wait()
    total = dot(mine[...], wo[...]) + dot(cross_mine[...], wco[...])
    finish(total, out, stage, sems, 0, done, odd, blocks)


def tail_kernel(
    band_in,
    factor_in,
    temp_in,
    align_in,
    counts_in,
    pack,
    near,
    context,
    wqkv,
    wckv,
    wo,
    wco,
    acc_in,
    sum_in,
    peak_in,
    q,
    cq,
    partial_out,
    out,
    band,
    factor,
    temp,
    align,
    counts,
    tokens,
    keys,
    vext,
    ck,
    cvext,
    mine,
    cross_mine,
    stage,
    sems,
):
    device = lax.axis_index("seq")
    odd = lax.rem(device, 2) == 1
    last = lax.axis_size("seq") - 1
    exists = jnp.where(odd, device < last, device > 0)
    rows, qwidth = q.shape
    blocks = rows // BLK
    halo = WMAX * BLK
    done = blocks - WMAX
    cwidth = context.shape[1]
    window = tokens.shape[0]

    scalars = scalar_copies(
        (band_in, factor_in, temp_in, align_in, counts_in),
        (band, factor, temp, align, counts),
        sems,
        WMAX,
    )
    vext[:, :, LANES:] = jnp.ones((vext.shape[0], vext.shape[1], LANES), BF16)
    cvext[:, :, LANES:] = jnp.ones((cvext.shape[0], cvext.shape[1], LANES), BF16)
    tokens[RCH * TOKB : RCH * TOKB + context.shape[0], :] = context[...]
    ends = [jnp.where(odd, 0, window - RCH * TOKB), jnp.where(odd, window - RCH * TOKB, 0)]
    for start, source in zip(ends, (near, pack)):
        at = pl.ds(pl.multiple_of(start, 16), RCH * TOKB)
        tokens[at, :] = unpack_tokens(source, halo, cwidth)

    def project(first, start):
        def begin():
            return dot(pack[first : first + TILE, :], wqkv[:, start : start + CHUNK])

        def end(x):
            part, col = divmod(start, qwidth)
            at = slice(first, first + TILE)
            if part == 1:
                keys[at, col : col + CHUNK] = head_norm(x)
            else:
                store_values(vext, at, col, x.astype(BF16))

        return begin, end

    staggered(
        [
            project(first, start)
            for start in range(qwidth, 3 * qwidth, CHUNK)
            for first in range(0, halo, TILE)
        ]
    )
    token_pairs(tokens, wckv, ck, cvext)
    for copy in scalars:
        copy.wait()

    def self_item(pair, f, shifted):
        heads = [2 * pair, 2 * pair + 1]
        lanes = lanes_of(pair)
        inner = blocks - 1 - f
        count = WMAX - inner
        start = pl.multiple_of(local_block(f, odd, blocks) * BLK, BLK)
        first = pl.multiple_of(jnp.where(odd, 0, halo - count * BLK), BLK)
        at = pl.ds(first, count * BLK)

        def begin():
            return pair_scores(q[pl.ds(start, BLK), lanes], keys[at, lanes])

        def end(scores):
            bias = [[] for _ in heads]
            for mine_bias, h in zip(bias, heads):
                width = jnp.where(exists, band[h], 0)
                for t in range(count):
                    one, two = band_bias(width, inner + 1 + t), band_bias(width, inner + count - t)
                    mine_bias.append(jnp.where(odd, one, two))
            scales = [factor[h] * (HD**-0.5 * LOG2E) for h in heads]
            part, weight, shifts = pair_sums(scores, vext[pair, at, :], scales, bias, shifted)
            to = slice((f - done) * BLK, (f - done + 1) * BLK)
            had, had_weight = acc_in[to, lanes], sum_in[to, lanes]
            if shifted:
                low = low_half(BLK)
                lane = lax.broadcasted_iota(jnp.int32, (BLK, LANES), 1)
                olds = [
                    jnp.sum(jnp.where(lane == h, peak_in[to, :], 0.0), axis=1, keepdims=True)
                    for h in heads
                ]
                news = [jnp.maximum(a, b) for a, b in zip(olds, shifts)]
                keep = [jnp.exp2(a - n) for a, n in zip(olds, news)]
                add = [jnp.exp2(b - n) for b, n in zip(shifts, news)]
                keep = jnp.where(low, keep[0], keep[1])
                add = jnp.where(low, add[0], add[1])
                had, had_weight = had * keep, had_weight * keep
                part, weight = part * add, weight * add
            mine[to, lanes] = ((had + part) / (had_weight + weight)).astype(BF16)

        return begin, end

    biases = [
        token_bias(
            align,
            counts,
            local_block(f, odd, blocks),
            device * (context.shape[0] // TOKB) - RCH,
            window,
        )
        for f in range(done, blocks)
    ]

    def cross_item(pair, f, shifted):
        lanes = lanes_of(pair)
        start = pl.multiple_of(local_block(f, odd, blocks) * BLK, BLK)

        def begin():
            return pair_scores(cq[pl.ds(start, BLK), lanes], ck[:, lanes])

        def end(scores):
            scales = [temp[2 * pair + i] * (HD**-0.5 * LOG2E) for i in range(2)]
            part, weight, _ = pair_sums(
                scores, cvext[pair], scales, [[biases[f - done]]] * 2, shifted
            )
            to = slice((f - done) * BLK, (f - done + 1) * BLK)
            cross_mine[to, lanes] = (part / weight).astype(BF16)

        return begin, end

    pairs, cross_pairs = qwidth // LANES, cwidth // LANES
    easy = plain(factor, temp)

    @pl.when(easy)
    def _():
        items = [
            cross_item(p, f, False) for p in range(cross_pairs) for f in range(done, blocks)
        ]
        items += [self_item(p, f, False) for p in range(pairs) for f in range(done, blocks)]
        staggered(items, 2)

    @pl.when(jnp.logical_not(easy))
    def _():
        @pl.loop(0, pairs)
        def _(p):
            staggered([self_item(p, f, True) for f in range(done, blocks)])

        @pl.loop(0, cross_pairs)
        def _(p):
            staggered([cross_item(p, f, True) for f in range(done, blocks)])

    total = dot(mine[...], wo[...]) + dot(cross_mine[...], wco[...])
    finish(total, out, stage, sems, done, WMAX, odd, blocks)


def shards(
    frames,
    context,
    noise_level,
    alignment,
    counts,
    band_width,
    mod_table,
    qkv_weight,
    out_weight,
    cross_query_weight,
    cross_kv_weight,
    cross_out_weight,
    banded_attender_factor,
    cross_temp,
):
    rows, width = frames.shape
    blocks = rows // BLK
    halo = WMAX * BLK
    done = blocks - WMAX
    tokens, cwidth = context.shape
    qwidth = qkv_weight.shape[1] // 3
    cqwidth = cross_query_weight.shape[1]
    pairs, cross_pairs = qwidth // LANES, cqwidth // LANES
    window = tokens + 2 * RCH * TOKB
    devices = lax.axis_size("seq")
    smem = pl.BlockSpec(memory_space=pltpu.SMEM)
    vmem = pl.BlockSpec(memory_space=pltpu.VMEM)
    hbm = pl.BlockSpec(memory_space=pltpu.HBM)
    pack_rows = halo + TOK_PACK

    hidden, near, far = pl.pallas_call(
        hidden_kernel,
        out_shape=[
            jax.ShapeDtypeStruct((rows, width), BF16),
            jax.ShapeDtypeStruct((pack_rows, width), BF16),
            jax.ShapeDtypeStruct((pack_rows, width), BF16),
        ],
        in_specs=[smem, hbm, vmem, vmem],
        out_specs=[vmem, vmem, vmem],
        scratch_shapes=[
            pltpu.VMEM((rows, width), BF16),
            pltpu.SemaphoreType.DMA((blocks,)),
        ],
        compiler_params=pltpu.CompilerParams(vmem_limit_bytes=8 * 2**20),
        name="hidden_and_packs",
    )(*in_hbm(noise_level, frames, mod_table, context))

    same_chip = [(i, i ^ 1) for i in range(devices) if i ^ 1 < devices]
    across = [(i, i + 1) for i in range(1, devices - 1, 2)]
    across += [(b, a) for a, b in across]
    far_got = lax.ppermute(far, "seq", across)
    near_got = lax.ppermute(near, "seq", same_chip)

    open_rows = WMAX * BLK
    scalar_scratch = [
        pltpu.SMEM(band_width.shape, jnp.int32),
        pltpu.SMEM(banded_attender_factor.shape, F32),
        pltpu.SMEM(cross_temp.shape, F32),
        pltpu.SMEM(alignment.shape[::-1], jnp.int32),
        pltpu.SMEM(counts.shape, jnp.int32),
    ]
    scalars = in_hbm(band_width, banded_attender_factor, cross_temp, alignment.T, counts)
    loads = 3 * qwidth // CHUNK + 4
    update, acc, weight, peaks, q, cq = pl.pallas_call(
        main_kernel,
        out_shape=[
            jax.ShapeDtypeStruct((rows, width), BF16),
            jax.ShapeDtypeStruct((open_rows, qwidth), F32),
            jax.ShapeDtypeStruct((open_rows, qwidth), F32),
            jax.ShapeDtypeStruct((open_rows, LANES), F32),
            jax.ShapeDtypeStruct((rows, qwidth), BF16),
            jax.ShapeDtypeStruct((rows, cqwidth), BF16),
        ],
        in_specs=[hbm] * 5 + [vmem] * 3 + [hbm] * 5,
        out_specs=[hbm] + [vmem] * 5,
        scratch_shapes=scalar_scratch
        + [
            pltpu.VMEM(qkv_weight.shape, BF16),
            pltpu.VMEM(cross_query_weight.shape, BF16),
            pltpu.VMEM(cross_kv_weight.shape, BF16),
            pltpu.VMEM(out_weight.shape, BF16),
            pltpu.VMEM(cross_out_weight.shape, BF16),
            pltpu.VMEM((window, cwidth), BF16),
            pltpu.VMEM((rows + halo, qwidth), BF16),
            pltpu.VMEM((pairs, rows + halo, 2 * LANES), BF16),
            pltpu.VMEM((window, cqwidth), BF16),
            pltpu.VMEM((cross_pairs, window, 2 * LANES), BF16),
            pltpu.VMEM((done * BLK, qwidth), BF16),
            pltpu.VMEM((done * BLK, cqwidth), BF16),
            pltpu.VMEM((done * BLK, width), BF16),
            pltpu.SemaphoreType.DMA((loads + 5,)),
        ],
        compiler_params=pltpu.CompilerParams(vmem_limit_bytes=MAIN_VMEM),
        cost_estimate=pl.CostEstimate(
            flops=12 * 10**9, bytes_accessed=20 * 10**6, transcendentals=5 * 10**6
        ),
        name="local_attention",
    )(
        *scalars,
        hidden,
        near_got,
        *in_hbm(
            context,
            qkv_weight,
            cross_query_weight,
            cross_kv_weight,
            out_weight,
            cross_out_weight,
        ),
    )

    return pl.pallas_call(
        tail_kernel,
        out_shape=jax.ShapeDtypeStruct((rows, width), BF16),
        in_specs=[hbm] * 5 + [vmem] * 12 + [hbm],
        out_specs=hbm,
        scratch_shapes=scalar_scratch
        + [
            pltpu.VMEM((window, cwidth), BF16),
            pltpu.VMEM((halo, qwidth), BF16),
            pltpu.VMEM((pairs, halo, 2 * LANES), BF16),
            pltpu.VMEM((window, cqwidth), BF16),
            pltpu.VMEM((cross_pairs, window, 2 * LANES), BF16),
            pltpu.VMEM((open_rows, qwidth), BF16),
            pltpu.VMEM((open_rows, cqwidth), BF16),
            pltpu.VMEM((open_rows, width), BF16),
            pltpu.SemaphoreType.DMA((WMAX + 5,)),
        ],
        input_output_aliases={17: 0},
        compiler_params=pltpu.CompilerParams(vmem_limit_bytes=TAIL_VMEM),
        cost_estimate=pl.CostEstimate(
            flops=5 * 10**9, bytes_accessed=12 * 10**6, transcendentals=10**6
        ),
        name="halo_attention",
    )(
        *scalars,
        far_got,
        near_got,
        *in_hbm(context),
        qkv_weight,
        cross_kv_weight,
        out_weight,
        cross_out_weight,
        acc,
        weight,
        peaks,
        q,
        cq,
        update,
    )


def solution(mesh):
    placed = (
        P(("groups", "seq"), None),
        P(("groups", "seq"), None),
        P(("groups", "seq")),
        P(("groups", "seq"), None),
        P(("groups", "seq")),
        P(),
        P(),
        P(),
        P(),
        P(),
        P(),
        P(),
        P(),
        P(),
    )
    return jax.shard_map(
        shards, mesh=mesh, in_specs=placed, out_specs=P(("groups", "seq"), None), check_vma=False
    )
```

```python
import jax
import jax.numpy as jnp
from jax import lax
from jax.experimental import pallas as pl
from jax.experimental.pallas import tpu as pltpu
from jax.sharding import PartitionSpec as P

BANDED_ATTEND_CT = 16
MIXED_ATTEND_CNT = 8
HD = 64
LEVELS = 8
BLK = 128
WMAX = 2
TOKB = 48
RCH = 1
ALIST = 2

LANES = 128
CHUNK = 512
TILE = 256
LOG2E = 1.4426950408889634
OFF = -1e30
PLAIN_FACTOR = 8.0
F32 = jnp.float32
BF16 = jnp.bfloat16
MAIN_VMEM = 24 * 2**20
TAIL_VMEM = 16 * 2**20
TOK_PACK = 32


def dot(a, b):
    return jnp.dot(a, b, preferred_element_type=F32)


def dot_t(a, b):
    return lax.dot_general(a, b, (((1,), (1,)), ((), ())), preferred_element_type=F32)


def low_half(rows):
    return lax.broadcasted_iota(jnp.int32, (rows, LANES), 1) < HD


def head_norm(x):
    low = low_half(x.shape[0])
    done = []
    for start in range(0, x.shape[1], LANES):
        pair = x[:, start : start + LANES]
        square = pair * pair
        first = jnp.sum(jnp.where(low, square, 0.0), axis=1, keepdims=True)
        second = jnp.sum(jnp.where(low, 0.0, square), axis=1, keepdims=True)
        mean = jnp.where(low, first, second) * (1.0 / HD)
        done.append((pair * lax.rsqrt(mean + 1e-06)).astype(BF16))
    return jnp.concatenate(done, 1)


def staggered(items, delay=1):
    begun = []
    for begin, end in items:
        begun.append((end, begin()))
        if len(begun) > delay:
            end, value = begun.pop(0)
            end(value)
    for end, value in begun:
        end(value)


def pair_scores(q, k):
    low = low_half(q.shape[0])
    zero = jnp.zeros_like(q)
    stacked = jnp.concatenate([jnp.where(low, q, zero), jnp.where(low, zero, q)], 0)
    return dot_t(stacked, k)


def pair_sums(scores, vext, scales, tile_bias, shifted):
    rows = scores.shape[0] // 2
    parts, shifts = [], []
    for head in range(2):
        mine = scores[head * rows : (head + 1) * rows]
        biases = tile_bias[head]
        width = mine.shape[1] // len(biases)
        tiles = []
        for t, bias in enumerate(biases):
            tile = mine[:, t * width : (t + 1) * width] * scales[head]
            tiles.append(tile if bias is None else tile + bias)
        if shifted:
            peak = tiles[0]
            for tile in tiles[1:]:
                peak = jnp.maximum(peak, tile)
            peak = jnp.max(peak, axis=1, keepdims=True)
            shifts.append(peak)
            tiles = [tile - peak for tile in tiles]
        tiles = [jnp.exp2(tile).astype(BF16) for tile in tiles]
        parts.append(tiles[0] if len(tiles) == 1 else jnp.concatenate(tiles, 1))
    got = dot(jnp.concatenate(parts, 0), vext)
    low = low_half(rows)
    total = jnp.where(low, got[:rows, :LANES], got[rows:, :LANES])
    weight = jnp.where(low, got[:rows, LANES:], got[rows:, LANES:])
    return total, weight, shifts


def band_bias(width, distance):
    return jnp.where(width >= distance, 0.0, OFF).astype(F32)


def plain(factor, temp):
    flag = factor[0] <= PLAIN_FACTOR
    for i in range(1, BANDED_ATTEND_CT):
        flag = flag & (factor[i] <= PLAIN_FACTOR)
    for i in range(MIXED_ATTEND_CNT):
        flag = flag & (temp[i] <= PLAIN_FACTOR)
    return flag


def token_bias(align, counts, block, first_token_block, window):
    place = lax.broadcasted_iota(jnp.int32, (1, window), 1) // TOKB + first_token_block
    allowed = place == align[0, block]
    for slot in range(1, ALIST):
        live = jnp.where(slot < counts[block], align[slot, block], -RCH - 1)
        allowed = allowed | (place == live)
    return jnp.where(allowed, 0.0, OFF).astype(F32)


def local_block(f, odd, blocks):
    return jnp.where(odd, f, blocks - 1 - f)


def in_hbm(*arrays):
    return [pltpu.with_memory_space_constraint(a, pltpu.HBM) for a in arrays]


def lanes_of(pair):
    if isinstance(pair, int):
        return slice(pair * LANES, (pair + 1) * LANES)
    return pl.ds(pl.multiple_of(pair * LANES, LANES), LANES)


def hidden_kernel(
    level_in,
    frames,
    table_in,
    context_in,
    wqkv,
    hidden,
    near,
    far,
    context,
    wqk,
    level,
    table,
    stage,
    sems,
):
    odd = lax.rem(lax.axis_index("seq"), 2) == 1
    rows, width = frames.shape
    blocks = rows // BLK
    loads = [(level_in, level), (table_in, table)]
    loads += [
        (frames.at[pl.ds(b * BLK, BLK)], stage.at[pl.ds(b * BLK, BLK)]) for b in range(blocks)
    ]
    loads.append((context_in, context))
    for start in range(0, wqk.shape[1], CHUNK):
        cols = pl.ds(start, CHUNK)
        loads.append((wqkv.at[:, cols], wqk.at[:, cols]))
    loads = [pltpu.make_async_copy(a, b, sems.at[i]) for i, (a, b) in enumerate(loads)]
    for load in loads:
        load.start()
    loads[0].wait()
    loads[1].wait()
    for b in range(blocks):
        at = pl.ds(b * BLK, BLK)
        row = table[pl.ds(level[b], 1), :]
        loads[2 + b].wait()
        x = stage[at, :].astype(F32)
        x = x * lax.rsqrt(jnp.mean(x * x, axis=1, keepdims=True) + 1e-06)
        hidden[at, :] = (x * (1.0 + row[:, :width]) + row[:, width:]).astype(BF16)
    loads[2 + blocks].wait()
    halo = WMAX * BLK
    tokens = context.shape[0]
    cwidth = context.shape[1]
    for pack, high in ((near, jnp.logical_not(odd)), (far, odd)):
        start = pl.multiple_of(jnp.where(high, rows - halo, 0), BLK)
        pack[:halo, :] = hidden[pl.ds(start, halo), :]
        start = pl.multiple_of(jnp.where(high, tokens - RCH * TOKB, 0), 16)
        tok = context[pl.ds(start, RCH * TOKB), :]
        pack[halo:, :cwidth] = tok[:TOK_PACK]
        pack[halo : halo + 16, cwidth:] = tok[TOK_PACK:]
        pack[halo + 16 :, cwidth:] = jnp.zeros((TOK_PACK - 16, cwidth), BF16)
    for load in loads[3 + blocks :]:
        load.wait()


def unpack_tokens(pack, halo, cwidth):
    return jnp.concatenate(
        [pack[halo : halo + TOK_PACK, :cwidth], pack[halo : halo + 16, cwidth:]], 0
    )


def token_pairs(tokens, wckv, ck, cvext):
    cwidth = ck.shape[1]
    x = tokens[...]
    ck[...] = head_norm(dot(x, wckv[:, :cwidth]))
    values = dot(x, wckv[:, cwidth:]).astype(BF16)
    for pair in range(cwidth // LANES):
        cvext[pair, :, :LANES] = values[:, lanes_of(pair)]


def store_values(vext, at, start, values):
    for i in range(values.shape[1] // LANES):
        vext[start // LANES + i, at, :LANES] = values[:, lanes_of(i)]


def scalar_copies(sources, targets, sems, first):
    copies = []
    for i, (source, target) in enumerate(zip(sources, targets)):
        copies.append(pltpu.make_async_copy(source, target, sems.at[first + i]))
        copies[-1].start()
    return copies


def finish(total, out, stage, sems, first, count, odd, blocks):
    copies = []
    for i in range(count):
        at = pl.ds(i * BLK, BLK)
        stage[at, :] = total[i * BLK : (i + 1) * BLK].astype(BF16)
        to = pl.multiple_of(local_block(first + i, odd, blocks) * BLK, BLK)
        copies.append(
            pltpu.make_async_copy(stage.at[at], out.at[pl.ds(to, BLK)], sems.at[i])
        )
        copies[-1].start()
    return copies


def main_kernel(
    band_in,
    factor_in,
    temp_in,
    align_in,
    counts_in,
    hidden,
    near,
    context,
    wqk,
    wqkv_in,
    wcq_in,
    wckv_in,
    wo_in,
    wco_in,
    out,
    acc_out,
    sum_out,
    peak_out,
    q,
    cq,
    wv,
    wckv,
    wo,
    wco,
    band,
    factor,
    temp,
    align,
    counts,
    wcq,
    tokens,
    keys,
    vext,
    ck,
    cvext,
    mine,
    cross_mine,
    stage,
    sems,
):
    device = lax.axis_index("seq")
    odd = lax.rem(device, 2) == 1
    rows = hidden.shape[0]
    blocks = rows // BLK
    halo = WMAX * BLK
    done = blocks - WMAX
    qwidth = q.shape[1]
    cwidth = context.shape[1]
    own = jnp.where(odd, halo, 0)
    other = jnp.where(odd, 0, rows)

    loads = []
    for start in range(0, qwidth, CHUNK):
        loads.append(
            (wqkv_in.at[:, pl.ds(2 * qwidth + start, CHUNK)], wv.at[:, pl.ds(start, CHUNK)])
        )
    loads += [(wcq_in, wcq), (wckv_in, wckv), (wo_in, wo), (wco_in, wco)]
    loads = [pltpu.make_async_copy(a, b, sems.at[i]) for i, (a, b) in enumerate(loads)]
    scalars = scalar_copies(
        (band_in, factor_in, temp_in, align_in, counts_in),
        (band, factor, temp, align, counts),
        sems,
        len(loads),
    )
    for load in loads:
        load.start()

    vext[:, :, LANES:] = jnp.ones((vext.shape[0], vext.shape[1], LANES), BF16)
    cvext[:, :, LANES:] = jnp.ones((cvext.shape[0], cvext.shape[1], LANES), BF16)
    tokens[...] = jnp.zeros_like(tokens)
    tokens[RCH * TOKB : RCH * TOKB + context.shape[0], :] = context[...]
    start = jnp.where(odd, 0, RCH * TOKB + context.shape[0])
    tokens[pl.ds(pl.multiple_of(start, 16), RCH * TOKB), :] = unpack_tokens(near, halo, cwidth)

    def project(source, first, to, start):
        def begin():
            part, col = divmod(start, qwidth)
            weight = wv if part == 2 else wqk
            col = col if part == 2 else start
            return dot(source[first : first + TILE, :], weight[:, col : col + CHUNK])

        def end(x):
            at = pl.ds(pl.multiple_of(to + first, BLK), TILE)
            part, col = divmod(start, qwidth)
            if part == 0:
                q[first : first + TILE, col : col + CHUNK] = head_norm(x)
            elif part == 1:
                keys[at, col : col + CHUNK] = head_norm(x)
            else:
                store_values(vext, at, col, x.astype(BF16))

        return begin, end

    def project_cross(first):
        def begin():
            return dot(hidden[first : first + TILE, :], wcq[...])

        def end(x):
            cq[first : first + TILE, :] = head_norm(x)

        return begin, end

    items = []
    for start in range(0, 3 * qwidth, CHUNK):
        tiles = [project(hidden, first, own, start) for first in range(0, rows, TILE)]
        if start >= qwidth:
            tiles += [project(near, first, other, start) for first in range(0, halo, TILE)]
        if start >= 2 * qwidth:
            load = loads[(start - 2 * qwidth) // CHUNK]
            begin, end = tiles[0]
            tiles[0] = (lambda load=load, begin=begin: (load.wait(), begin())[1], end)
        items += tiles
    staggered(items)
    count = qwidth // CHUNK
    loads[count].wait()
    loads[count + 1].wait()
    staggered([project_cross(first) for first in range(0, rows, TILE)])
    token_pairs(tokens, wckv, ck, cvext)
    for copy in scalars:
        copy.wait()

    def self_item(pair, f, shifted):
        heads = [2 * pair, 2 * pair + 1]
        lanes = lanes_of(pair)
        inner = min(WMAX, blocks - 1 - f)
        count = WMAX + 1 + inner
        start = pl.multiple_of(local_block(f, odd, blocks) * BLK, BLK)
        first = pl.multiple_of(jnp.where(odd, f, blocks - 1 - f - inner) * BLK, BLK)
        at = pl.ds(first, count * BLK)

        def begin():
            return pair_scores(q[pl.ds(start, BLK), lanes], keys[at, lanes])

        def end(scores):
            bias = [[] for _ in heads]
            for mine_bias, h in zip(bias, heads):
                by_distance = [0.0] + [band_bias(band[h], d) for d in range(1, WMAX + 1)]
                for t in range(count):
                    one, two = abs(t - WMAX), abs(t - inner)
                    if one == two:
                        mine_bias.append(None if one == 0 else by_distance[one])
                    else:
                        mine_bias.append(jnp.where(odd, by_distance[one], by_distance[two]))
            scales = [factor[h] * (HD**-0.5 * LOG2E) for h in heads]
            part, weight, shifts = pair_sums(scores, vext[pair, at, :], scales, bias, shifted)
            if f < done:
                mine[f * BLK : (f + 1) * BLK, lanes] = (part / weight).astype(BF16)
                return
            to = slice((f - done) * BLK, (f - done + 1) * BLK)
            acc_out[to, lanes] = part
            sum_out[to, lanes] = weight
            if shifted:
                lane = lax.broadcasted_iota(jnp.int32, (BLK, LANES), 1)
                peaks = peak_out[to, :]
                for h, shift in zip(heads, shifts):
                    peaks = jnp.where(lane == h, shift, peaks)
                peak_out[to, :] = peaks

        return begin, end

    biases = [
        token_bias(
            align,
            counts,
            local_block(f, odd, blocks),
            device * (context.shape[0] // TOKB) - RCH,
            tokens.shape[0],
        )
        for f in range(done)
    ]

    def cross_item(pair, f, shifted):
        lanes = lanes_of(pair)
        start = pl.multiple_of(local_block(f, odd, blocks) * BLK, BLK)

        def begin():
            return pair_scores(cq[pl.ds(start, BLK), lanes], ck[:, lanes])

        def end(scores):
            scales = [temp[2 * pair + i] * (HD**-0.5 * LOG2E) for i in range(2)]
            part, weight, _ = pair_sums(
                scores, cvext[pair], scales, [[biases[f]]] * 2, shifted
            )
            cross_mine[f * BLK : (f + 1) * BLK, lanes] = (part / weight).astype(BF16)

        return begin, end

    pairs, cross_pairs = qwidth // LANES, cwidth // LANES
    easy = plain(factor, temp)

    def project_out():
        for load in loads[count + 2 :]:
            load.wait()
        total = dot(mine[...], wo[...]) + dot(cross_mine[...], wco[...])
        return finish(total, out, stage, sems, 0, done, odd, blocks)

    @pl.when(easy)
    def _():
        items = [cross_item(p, f, False) for p in range(cross_pairs) for f in range(done)]
        items += [self_item(p, f, False) for p in range(pairs) for f in range(done)]
        staggered(items)
        copies = project_out()
        staggered(
            [self_item(p, f, False) for p in range(pairs) for f in range(done, blocks)]
        )
        for copy in copies:
            copy.wait()

    @pl.when(jnp.logical_not(easy))
    def _():
        peak_out[...] = jnp.zeros_like(peak_out)

        @pl.loop(0, pairs)
        def _(p):
            staggered([self_item(p, f, True) for f in range(blocks)])

        @pl.loop(0, cross_pairs)
        def _(p):
            staggered([cross_item(p, f, True) for f in range(done)])

        for copy in project_out():
            copy.wait()


def tail_kernel(
    band_in,
    factor_in,
    temp_in,
    align_in,
    counts_in,
    pack,
    near,
    context,
    wqk,
    wv,
    wckv,
    wo,
    wco,
    acc_in,
    sum_in,
    peak_in,
    q,
    cq,
    partial_out,
    out,
    band,
    factor,
    temp,
    align,
    counts,
    tokens,
    keys,
    vext,
    ck,
    cvext,
    mine,
    cross_mine,
    stage,
    sems,
):
    device = lax.axis_index("seq")
    odd = lax.rem(device, 2) == 1
    last = lax.axis_size("seq") - 1
    exists = jnp.where(odd, device < last, device > 0)
    rows, qwidth = q.shape
    blocks = rows // BLK
    halo = WMAX * BLK
    done = blocks - WMAX
    cwidth = context.shape[1]
    window = tokens.shape[0]

    scalars = scalar_copies(
        (band_in, factor_in, temp_in, align_in, counts_in),
        (band, factor, temp, align, counts),
        sems,
        WMAX,
    )
    vext[:, :, LANES:] = jnp.ones((vext.shape[0], vext.shape[1], LANES), BF16)
    cvext[:, :, LANES:] = jnp.ones((cvext.shape[0], cvext.shape[1], LANES), BF16)
    tokens[RCH * TOKB : RCH * TOKB + context.shape[0], :] = context[...]
    ends = [jnp.where(odd, 0, window - RCH * TOKB), jnp.where(odd, window - RCH * TOKB, 0)]
    for start, source in zip(ends, (near, pack)):
        at = pl.ds(pl.multiple_of(start, 16), RCH * TOKB)
        tokens[at, :] = unpack_tokens(source, halo, cwidth)

    def project(first, start):
        def begin():
            part, col = divmod(start, qwidth)
            weight = wv if part == 2 else wqk
            col = col if part == 2 else start
            return dot(pack[first : first + TILE, :], weight[:, col : col + CHUNK])

        def end(x):
            part, col = divmod(start, qwidth)
            at = slice(first, first + TILE)
            if part == 1:
                keys[at, col : col + CHUNK] = head_norm(x)
            else:
                store_values(vext, at, col, x.astype(BF16))

        return begin, end

    staggered(
        [
            project(first, start)
            for start in range(qwidth, 3 * qwidth, CHUNK)
            for first in range(0, halo, TILE)
        ]
    )
    token_pairs(tokens, wckv, ck, cvext)
    for copy in scalars:
        copy.wait()

    def self_item(pair, f, shifted):
        heads = [2 * pair, 2 * pair + 1]
        lanes = lanes_of(pair)
        inner = blocks - 1 - f
        count = WMAX - inner
        start = pl.multiple_of(local_block(f, odd, blocks) * BLK, BLK)
        first = pl.multiple_of(jnp.where(odd, 0, halo - count * BLK), BLK)
        at = pl.ds(first, count * BLK)

        def begin():
            return pair_scores(q[pl.ds(start, BLK), lanes], keys[at, lanes])

        def end(scores):
            bias = [[] for _ in heads]
            for mine_bias, h in zip(bias, heads):
                width = jnp.where(exists, band[h], 0)
                for t in range(count):
                    one, two = band_bias(width, inner + 1 + t), band_bias(width, inner + count - t)
                    mine_bias.append(jnp.where(odd, one, two))
            scales = [factor[h] * (HD**-0.5 * LOG2E) for h in heads]
            part, weight, shifts = pair_sums(scores, vext[pair, at, :], scales, bias, shifted)
            to = slice((f - done) * BLK, (f - done + 1) * BLK)
            had, had_weight = acc_in[to, lanes], sum_in[to, lanes]
            if shifted:
                low = low_half(BLK)
                lane = lax.broadcasted_iota(jnp.int32, (BLK, LANES), 1)
                olds = [
                    jnp.sum(jnp.where(lane == h, peak_in[to, :], 0.0), axis=1, keepdims=True)
                    for h in heads
                ]
                news = [jnp.maximum(a, b) for a, b in zip(olds, shifts)]
                keep = [jnp.exp2(a - n) for a, n in zip(olds, news)]
                add = [jnp.exp2(b - n) for b, n in zip(shifts, news)]
                keep = jnp.where(low, keep[0], keep[1])
                add = jnp.where(low, add[0], add[1])
                had, had_weight = had * keep, had_weight * keep
                part, weight = part * add, weight * add
            mine[to, lanes] = ((had + part) / (had_weight + weight)).astype(BF16)

        return begin, end

    biases = [
        token_bias(
            align,
            counts,
            local_block(f, odd, blocks),
            device * (context.shape[0] // TOKB) - RCH,
            window,
        )
        for f in range(done, blocks)
    ]

    def cross_item(pair, f, shifted):
        lanes = lanes_of(pair)
        start = pl.multiple_of(local_block(f, odd, blocks) * BLK, BLK)

        def begin():
            return pair_scores(cq[pl.ds(start, BLK), lanes], ck[:, lanes])

        def end(scores):
            scales = [temp[2 * pair + i] * (HD**-0.5 * LOG2E) for i in range(2)]
            part, weight, _ = pair_sums(
                scores, cvext[pair], scales, [[biases[f - done]]] * 2, shifted
            )
            to = slice((f - done) * BLK, (f - done + 1) * BLK)
            cross_mine[to, lanes] = (part / weight).astype(BF16)

        return begin, end

    pairs, cross_pairs = qwidth // LANES, cwidth // LANES
    easy = plain(factor, temp)

    @pl.when(easy)
    def _():
        items = [
            cross_item(p, f, False) for p in range(cross_pairs) for f in range(done, blocks)
        ]
        items += [self_item(p, f, False) for p in range(pairs) for f in range(done, blocks)]
        staggered(items, 2)

    @pl.when(jnp.logical_not(easy))
    def _():
        @pl.loop(0, pairs)
        def _(p):
            staggered([self_item(p, f, True) for f in range(done, blocks)])

        @pl.loop(0, cross_pairs)
        def _(p):
            staggered([cross_item(p, f, True) for f in range(done, blocks)])

    total = dot(mine[...], wo[...]) + dot(cross_mine[...], wco[...])
    for copy in finish(total, out, stage, sems, done, WMAX, odd, blocks):
        copy.wait()


def shards(
    frames,
    context,
    noise_level,
    alignment,
    counts,
    band_width,
    mod_table,
    qkv_weight,
    out_weight,
    cross_query_weight,
    cross_kv_weight,
    cross_out_weight,
    banded_attender_factor,
    cross_temp,
):
    rows, width = frames.shape
    blocks = rows // BLK
    halo = WMAX * BLK
    done = blocks - WMAX
    tokens, cwidth = context.shape
    qwidth = qkv_weight.shape[1] // 3
    cqwidth = cross_query_weight.shape[1]
    pairs, cross_pairs = qwidth // LANES, cqwidth // LANES
    window = tokens + 2 * RCH * TOKB
    devices = lax.axis_size("seq")
    vmem = pl.BlockSpec(memory_space=pltpu.VMEM)
    hbm = pl.BlockSpec(memory_space=pltpu.HBM)
    pack_rows = halo + TOK_PACK

    hidden, near, far, context, wqk = pl.pallas_call(
        hidden_kernel,
        out_shape=[
            jax.ShapeDtypeStruct((rows, width), BF16),
            jax.ShapeDtypeStruct((pack_rows, width), BF16),
            jax.ShapeDtypeStruct((pack_rows, width), BF16),
            jax.ShapeDtypeStruct(context.shape, BF16),
            jax.ShapeDtypeStruct((width, 2 * qwidth), BF16),
        ],
        in_specs=[hbm] * 5,
        out_specs=[vmem] * 5,
        scratch_shapes=[
            pltpu.SMEM(noise_level.shape, jnp.int32),
            pltpu.VMEM(mod_table.shape, F32),
            pltpu.VMEM((rows, width), BF16),
            pltpu.SemaphoreType.DMA((blocks + 3 + 2 * qwidth // CHUNK,)),
        ],
        compiler_params=pltpu.CompilerParams(vmem_limit_bytes=8 * 2**20),
        name="hidden_and_packs",
    )(*in_hbm(noise_level, frames, mod_table, context, qkv_weight))

    same_chip = [(i, i ^ 1) for i in range(devices) if i ^ 1 < devices]
    across = [(i, i + 1) for i in range(1, devices - 1, 2)]
    across += [(b, a) for a, b in across]
    far_got = lax.ppermute(far, "seq", across)
    near_got = lax.ppermute(near, "seq", same_chip)

    open_rows = WMAX * BLK
    scalar_scratch = [
        pltpu.SMEM(band_width.shape, jnp.int32),
        pltpu.SMEM(banded_attender_factor.shape, F32),
        pltpu.SMEM(cross_temp.shape, F32),
        pltpu.SMEM(alignment.shape[::-1], jnp.int32),
        pltpu.SMEM(counts.shape, jnp.int32),
    ]
    scalars = in_hbm(band_width, banded_attender_factor, cross_temp, alignment.T, counts)
    loads = qwidth // CHUNK + 4
    update, acc, weight, peaks, q, cq, wv, wckv, wo, wco = pl.pallas_call(
        main_kernel,
        out_shape=[
            jax.ShapeDtypeStruct((rows, width), BF16),
            jax.ShapeDtypeStruct((open_rows, qwidth), F32),
            jax.ShapeDtypeStruct((open_rows, qwidth), F32),
            jax.ShapeDtypeStruct((open_rows, LANES), F32),
            jax.ShapeDtypeStruct((rows, qwidth), BF16),
            jax.ShapeDtypeStruct((rows, cqwidth), BF16),
            jax.ShapeDtypeStruct((width, qwidth), BF16),
            jax.ShapeDtypeStruct(cross_kv_weight.shape, BF16),
            jax.ShapeDtypeStruct(out_weight.shape, BF16),
            jax.ShapeDtypeStruct(cross_out_weight.shape, BF16),
        ],
        in_specs=[hbm] * 5 + [vmem] * 4 + [hbm] * 5,
        out_specs=[hbm] + [vmem] * 9,
        scratch_shapes=scalar_scratch
        + [
            pltpu.VMEM(cross_query_weight.shape, BF16),
            pltpu.VMEM((window, cwidth), BF16),
            pltpu.VMEM((rows + halo, qwidth), BF16),
            pltpu.VMEM((pairs, rows + halo, 2 * LANES), BF16),
            pltpu.VMEM((window, cqwidth), BF16),
            pltpu.VMEM((cross_pairs, window, 2 * LANES), BF16),
            pltpu.VMEM((done * BLK, qwidth), BF16),
            pltpu.VMEM((done * BLK, cqwidth), BF16),
            pltpu.VMEM((done * BLK, width), BF16),
            pltpu.SemaphoreType.DMA((loads + 5,)),
        ],
        compiler_params=pltpu.CompilerParams(vmem_limit_bytes=MAIN_VMEM),
        cost_estimate=pl.CostEstimate(
            flops=12 * 10**9, bytes_accessed=20 * 10**6, transcendentals=5 * 10**6
        ),
        name="local_attention",
    )(
        *scalars,
        hidden,
        near_got,
        context,
        wqk,
        *in_hbm(
            qkv_weight,
            cross_query_weight,
            cross_kv_weight,
            out_weight,
            cross_out_weight,
        ),
    )

    return pl.pallas_call(
        tail_kernel,
        out_shape=jax.ShapeDtypeStruct((rows, width), BF16),
        in_specs=[hbm] * 5 + [vmem] * 13 + [hbm],
        out_specs=hbm,
        scratch_shapes=scalar_scratch
        + [
            pltpu.VMEM((window, cwidth), BF16),
            pltpu.VMEM((halo, qwidth), BF16),
            pltpu.VMEM((pairs, halo, 2 * LANES), BF16),
            pltpu.VMEM((window, cqwidth), BF16),
            pltpu.VMEM((cross_pairs, window, 2 * LANES), BF16),
            pltpu.VMEM((open_rows, qwidth), BF16),
            pltpu.VMEM((open_rows, cqwidth), BF16),
            pltpu.VMEM((open_rows, width), BF16),
            pltpu.SemaphoreType.DMA((WMAX + 5,)),
        ],
        input_output_aliases={18: 0},
        compiler_params=pltpu.CompilerParams(vmem_limit_bytes=TAIL_VMEM),
        cost_estimate=pl.CostEstimate(
            flops=5 * 10**9, bytes_accessed=12 * 10**6, transcendentals=10**6
        ),
        name="halo_attention",
    )(
        *scalars,
        far_got,
        near_got,
        context,
        wqk,
        wv,
        wckv,
        wo,
        wco,
        acc,
        weight,
        peaks,
        q,
        cq,
        update,
    )


def solution(mesh):
    placed = (
        P(("groups", "seq"), None),
        P(("groups", "seq"), None),
        P(("groups", "seq")),
        P(("groups", "seq"), None),
        P(("groups", "seq")),
        P(),
        P(),
        P(),
        P(),
        P(),
        P(),
        P(),
        P(),
        P(),
    )
    return jax.shard_map(
        shards, mesh=mesh, in_specs=placed, out_specs=P(("groups", "seq"), None), check_vma=False
    )
```

```python
import jax
import jax.numpy as jnp
from jax import lax
from jax.experimental import pallas as pl
from jax.experimental.pallas import tpu as pltpu
from jax.sharding import PartitionSpec as P

BANDED_ATTEND_CT = 16
MIXED_ATTEND_CNT = 8
HD = 64
LEVELS = 8
BLK = 128
WMAX = 2
TOKB = 48
RCH = 1
ALIST = 2

LANES = 128
CHUNK = 512
TILE = 256
LOG2E = 1.4426950408889634
OFF = -1e30
PLAIN_FACTOR = 8.0
F32 = jnp.float32
BF16 = jnp.bfloat16
MAIN_VMEM = 24 * 2**20
TAIL_VMEM = 16 * 2**20
TOK_PACK = 32


def dot(a, b):
    return jnp.dot(a, b, preferred_element_type=F32)


def dot_t(a, b):
    return lax.dot_general(a, b, (((1,), (1,)), ((), ())), preferred_element_type=F32)


def low_half(rows):
    return lax.broadcasted_iota(jnp.int32, (rows, LANES), 1) < HD


def head_norm(x):
    low = low_half(x.shape[0])
    done = []
    for start in range(0, x.shape[1], LANES):
        pair = x[:, start : start + LANES]
        square = pair * pair
        first = jnp.sum(jnp.where(low, square, 0.0), axis=1, keepdims=True)
        second = jnp.sum(jnp.where(low, 0.0, square), axis=1, keepdims=True)
        mean = jnp.where(low, first, second) * (1.0 / HD)
        done.append((pair * lax.rsqrt(mean + 1e-06)).astype(BF16))
    return jnp.concatenate(done, 1)


def staggered(items, delay=1):
    begun = []
    for begin, end in items:
        begun.append((end, begin()))
        if len(begun) > delay:
            end, value = begun.pop(0)
            end(value)
    for end, value in begun:
        end(value)


def pair_scores(q, k):
    low = low_half(q.shape[0])
    zero = jnp.zeros_like(q)
    stacked = jnp.concatenate([jnp.where(low, q, zero), jnp.where(low, zero, q)], 0)
    return dot_t(stacked, k)


def pair_sums(scores, vext, scales, tile_bias, shifted):
    rows = scores.shape[0] // 2
    parts, shifts = [], []
    for head in range(2):
        mine = scores[head * rows : (head + 1) * rows]
        biases = tile_bias[head]
        width = mine.shape[1] // len(biases)
        tiles = []
        for t, bias in enumerate(biases):
            tile = mine[:, t * width : (t + 1) * width] * scales[head]
            tiles.append(tile if bias is None else tile + bias)
        if shifted:
            peak = tiles[0]
            for tile in tiles[1:]:
                peak = jnp.maximum(peak, tile)
            peak = jnp.max(peak, axis=1, keepdims=True)
            shifts.append(peak)
            tiles = [tile - peak for tile in tiles]
        tiles = [jnp.exp2(tile).astype(BF16) for tile in tiles]
        parts.append(tiles[0] if len(tiles) == 1 else jnp.concatenate(tiles, 1))
    got = dot(jnp.concatenate(parts, 0), vext)
    low = low_half(rows)
    total = jnp.where(low, got[:rows, :LANES], got[rows:, :LANES])
    weight = jnp.where(low, got[:rows, LANES:], got[rows:, LANES:])
    return total, weight, shifts


def band_bias(width, distance):
    return jnp.where(width >= distance, 0.0, OFF).astype(F32)


def plain(factor, temp):
    flag = factor[0] <= PLAIN_FACTOR
    for i in range(1, BANDED_ATTEND_CT):
        flag = flag & (factor[i] <= PLAIN_FACTOR)
    for i in range(MIXED_ATTEND_CNT):
        flag = flag & (temp[i] <= PLAIN_FACTOR)
    return flag


def token_bias(align, counts, block, first_token_block, window):
    place = lax.broadcasted_iota(jnp.int32, (1, window), 1) // TOKB + first_token_block
    allowed = place == align[0, block]
    for slot in range(1, ALIST):
        live = jnp.where(slot < counts[block], align[slot, block], -RCH - 1)
        allowed = allowed | (place == live)
    return jnp.where(allowed, 0.0, OFF).astype(F32)


def local_block(f, odd, blocks):
    return jnp.where(odd, f, blocks - 1 - f)


def in_hbm(*arrays):
    return [pltpu.with_memory_space_constraint(a, pltpu.HBM) for a in arrays]


def lanes_of(pair):
    if isinstance(pair, int):
        return slice(pair * LANES, (pair + 1) * LANES)
    return pl.ds(pl.multiple_of(pair * LANES, LANES), LANES)


def hidden_kernel(
    level_in,
    frames,
    table_in,
    context_in,
    hidden,
    near,
    far,
    context,
    level,
    table,
    stage,
    sems,
):
    odd = lax.rem(lax.axis_index("seq"), 2) == 1
    rows, width = frames.shape
    blocks = rows // BLK
    loads = [(level_in, level), (table_in, table)]
    loads += [
        (frames.at[pl.ds(b * BLK, BLK)], stage.at[pl.ds(b * BLK, BLK)]) for b in range(blocks)
    ]
    loads.append((context_in, context))
    loads = [pltpu.make_async_copy(a, b, sems.at[i]) for i, (a, b) in enumerate(loads)]
    for load in loads:
        load.start()
    loads[0].wait()
    loads[1].wait()
    for b in range(blocks):
        at = pl.ds(b * BLK, BLK)
        row = table[pl.ds(level[b], 1), :]
        loads[2 + b].wait()
        x = stage[at, :].astype(F32)
        x = x * lax.rsqrt(jnp.mean(x * x, axis=1, keepdims=True) + 1e-06)
        hidden[at, :] = (x * (1.0 + row[:, :width]) + row[:, width:]).astype(BF16)
    loads[2 + blocks].wait()
    halo = WMAX * BLK
    tokens = context.shape[0]
    cwidth = context.shape[1]
    for pack, high in ((near, jnp.logical_not(odd)), (far, odd)):
        start = pl.multiple_of(jnp.where(high, rows - halo, 0), BLK)
        pack[:halo, :] = hidden[pl.ds(start, halo), :]
        start = pl.multiple_of(jnp.where(high, tokens - RCH * TOKB, 0), 16)
        tok = context[pl.ds(start, RCH * TOKB), :]
        pack[halo:, :cwidth] = tok[:TOK_PACK]
        pack[halo : halo + 16, cwidth:] = tok[TOK_PACK:]
        pack[halo + 16 :, cwidth:] = jnp.zeros((TOK_PACK - 16, cwidth), BF16)
    for load in loads[3 + blocks :]:
        load.wait()


def unpack_tokens(pack, halo, cwidth):
    return jnp.concatenate(
        [pack[halo : halo + TOK_PACK, :cwidth], pack[halo : halo + 16, cwidth:]], 0
    )


def token_item(rows, start, wckv, ck, cvext):
    at = pl.ds(start, rows.shape[0])
    cwidth = ck.shape[1]

    def begin():
        return dot(rows[...], wckv[...])

    def end(x):
        ck[at, :] = head_norm(x[:, :cwidth])
        store_values(cvext, at, 0, x[:, cwidth:].astype(BF16))

    return begin, end


def store_values(vext, at, start, values):
    for i in range(values.shape[1] // LANES):
        vext[start // LANES + i, at, :LANES] = values[:, lanes_of(i)]


def scalar_copies(sources, targets, sems, first):
    copies = []
    for i, (source, target) in enumerate(zip(sources, targets)):
        copies.append(pltpu.make_async_copy(source, target, sems.at[first + i]))
        copies[-1].start()
    return copies


def finish(total, out, stage, sems, first, count, odd, blocks):
    copies = []
    for i in range(count):
        at = pl.ds(i * BLK, BLK)
        stage[at, :] = total[i * BLK : (i + 1) * BLK].astype(BF16)
        to = pl.multiple_of(local_block(first + i, odd, blocks) * BLK, BLK)
        copies.append(
            pltpu.make_async_copy(stage.at[at], out.at[pl.ds(to, BLK)], sems.at[i])
        )
        copies[-1].start()
    return copies


def main_kernel(
    band_in,
    factor_in,
    temp_in,
    align_in,
    counts_in,
    hidden,
    near,
    context,
    wqkv,
    wcq,
    wckv,
    wo_in,
    wco_in,
    out,
    acc_out,
    sum_out,
    peak_out,
    q,
    cq,
    wo,
    wco,
    ck,
    cvext,
    band,
    factor,
    temp,
    align,
    counts,
    tokens,
    keys,
    vext,
    mine,
    cross_mine,
    stage,
    sems,
):
    device = lax.axis_index("seq")
    odd = lax.rem(device, 2) == 1
    rows = hidden.shape[0]
    blocks = rows // BLK
    halo = WMAX * BLK
    done = blocks - WMAX
    qwidth = q.shape[1]
    cwidth = context.shape[1]
    own = jnp.where(odd, halo, 0)
    other = jnp.where(odd, 0, rows)

    loads = [(wo_in, wo), (wco_in, wco)]
    loads = [pltpu.make_async_copy(a, b, sems.at[i]) for i, (a, b) in enumerate(loads)]
    scalars = scalar_copies(
        (band_in, factor_in, temp_in, align_in, counts_in),
        (band, factor, temp, align, counts),
        sems,
        len(loads),
    )
    for load in loads:
        load.start()

    vext[:, :, LANES:] = jnp.ones((vext.shape[0], vext.shape[1], LANES), BF16)
    cvext[:, :, LANES:] = jnp.ones((cvext.shape[0], cvext.shape[1], LANES), BF16)
    tokens[...] = jnp.zeros_like(tokens)
    tokens[RCH * TOKB : RCH * TOKB + context.shape[0], :] = context[...]
    start = jnp.where(odd, 0, RCH * TOKB + context.shape[0])
    tokens[pl.ds(pl.multiple_of(start, 16), RCH * TOKB), :] = unpack_tokens(near, halo, cwidth)

    def project(source, first, to, start):
        def begin():
            return dot(source[first : first + TILE, :], wqkv[:, start : start + CHUNK])

        def end(x):
            at = pl.ds(pl.multiple_of(to + first, BLK), TILE)
            part, col = divmod(start, qwidth)
            if part == 0:
                q[first : first + TILE, col : col + CHUNK] = head_norm(x)
            elif part == 1:
                keys[at, col : col + CHUNK] = head_norm(x)
            else:
                store_values(vext, at, col, x.astype(BF16))

        return begin, end

    def project_cross(first):
        def begin():
            return dot(hidden[first : first + TILE, :], wcq[...])

        def end(x):
            cq[first : first + TILE, :] = head_norm(x)

        return begin, end

    items = []
    for start in range(0, 3 * qwidth, CHUNK):
        tiles = [project(hidden, first, own, start) for first in range(0, rows, TILE)]
        if start >= qwidth:
            tiles += [project(near, first, other, start) for first in range(0, halo, TILE)]
        items += tiles
    items += [project_cross(first) for first in range(0, rows, TILE)]
    items.append(token_item(tokens, 0, wckv, ck, cvext))
    staggered(items)
    for copy in scalars:
        copy.wait()

    def self_item(pair, f, shifted):
        heads = [2 * pair, 2 * pair + 1]
        lanes = lanes_of(pair)
        inner = min(WMAX, blocks - 1 - f)
        count = WMAX + 1 + inner
        start = pl.multiple_of(local_block(f, odd, blocks) * BLK, BLK)
        first = pl.multiple_of(jnp.where(odd, f, blocks - 1 - f - inner) * BLK, BLK)
        at = pl.ds(first, count * BLK)

        def begin():
            return pair_scores(q[pl.ds(start, BLK), lanes], keys[at, lanes])

        def end(scores):
            bias = [[] for _ in heads]
            for mine_bias, h in zip(bias, heads):
                by_distance = [0.0] + [band_bias(band[h], d) for d in range(1, WMAX + 1)]
                for t in range(count):
                    one, two = abs(t - WMAX), abs(t - inner)
                    if one == two:
                        mine_bias.append(None if one == 0 else by_distance[one])
                    else:
                        mine_bias.append(jnp.where(odd, by_distance[one], by_distance[two]))
            scales = [factor[h] * (HD**-0.5 * LOG2E) for h in heads]
            part, weight, shifts = pair_sums(scores, vext[pair, at, :], scales, bias, shifted)
            if f < done:
                mine[f * BLK : (f + 1) * BLK, lanes] = (part / weight).astype(BF16)
                return
            to = slice((f - done) * BLK, (f - done + 1) * BLK)
            acc_out[to, lanes] = part
            sum_out[to, lanes] = weight
            if shifted:
                lane = lax.broadcasted_iota(jnp.int32, (BLK, LANES), 1)
                peaks = peak_out[to, :]
                for h, shift in zip(heads, shifts):
                    peaks = jnp.where(lane == h, shift, peaks)
                peak_out[to, :] = peaks

        return begin, end

    biases = [
        token_bias(
            align,
            counts,
            local_block(f, odd, blocks),
            device * (context.shape[0] // TOKB) - RCH,
            tokens.shape[0],
        )
        for f in range(done)
    ]

    def cross_item(pair, f, shifted):
        lanes = lanes_of(pair)
        start = pl.multiple_of(local_block(f, odd, blocks) * BLK, BLK)

        def begin():
            return pair_scores(cq[pl.ds(start, BLK), lanes], ck[:, lanes])

        def end(scores):
            scales = [temp[2 * pair + i] * (HD**-0.5 * LOG2E) for i in range(2)]
            part, weight, _ = pair_sums(
                scores, cvext[pair], scales, [[biases[f]]] * 2, shifted
            )
            cross_mine[f * BLK : (f + 1) * BLK, lanes] = (part / weight).astype(BF16)

        return begin, end

    pairs, cross_pairs = qwidth // LANES, cwidth // LANES
    easy = plain(factor, temp)

    def project_out():
        for load in loads:
            load.wait()
        total = dot(mine[...], wo[...]) + dot(cross_mine[...], wco[...])
        return finish(total, out, stage, sems, 0, done, odd, blocks)

    @pl.when(easy)
    def _():
        items = [cross_item(p, f, False) for p in range(cross_pairs) for f in range(done)]
        items += [self_item(p, f, False) for p in range(pairs) for f in range(done)]
        staggered(items)
        copies = project_out()
        staggered(
            [self_item(p, f, False) for p in range(pairs) for f in range(done, blocks)]
        )
        for copy in copies:
            copy.wait()

    @pl.when(jnp.logical_not(easy))
    def _():
        peak_out[...] = jnp.zeros_like(peak_out)

        @pl.loop(0, pairs)
        def _(p):
            staggered([self_item(p, f, True) for f in range(blocks)])

        @pl.loop(0, cross_pairs)
        def _(p):
            staggered([cross_item(p, f, True) for f in range(done)])

        for copy in project_out():
            copy.wait()


def tail_kernel(
    band_in,
    factor_in,
    temp_in,
    align_in,
    counts_in,
    pack,
    wqkv,
    wo,
    wco,
    wckv,
    ck_in,
    cvext_in,
    acc_in,
    sum_in,
    peak_in,
    q,
    cq,
    partial_out,
    out,
    band,
    factor,
    temp,
    align,
    counts,
    late,
    keys,
    vext,
    ck,
    cvext,
    mine,
    cross_mine,
    stage,
    sems,
):
    device = lax.axis_index("seq")
    odd = lax.rem(device, 2) == 1
    last = lax.axis_size("seq") - 1
    exists = jnp.where(odd, device < last, device > 0)
    rows, qwidth = q.shape
    blocks = rows // BLK
    halo = WMAX * BLK
    done = blocks - WMAX
    window, cwidth = ck.shape
    tokens = window - 2 * RCH * TOKB

    scalars = scalar_copies(
        (band_in, factor_in, temp_in, align_in, counts_in),
        (band, factor, temp, align, counts),
        sems,
        WMAX,
    )
    vext[:, :, LANES:] = jnp.ones((vext.shape[0], vext.shape[1], LANES), BF16)
    ck[...] = ck_in[...]
    cvext[...] = cvext_in[...]
    late[...] = unpack_tokens(pack, halo, wckv.shape[0])
    late_at = pl.multiple_of(jnp.where(odd, window - RCH * TOKB, 0), 16)

    def project(first, start):
        def begin():
            return dot(pack[first : first + TILE, :], wqkv[:, start : start + CHUNK])

        def end(x):
            part, col = divmod(start, qwidth)
            at = slice(first, first + TILE)
            if part == 1:
                keys[at, col : col + CHUNK] = head_norm(x)
            else:
                store_values(vext, at, col, x.astype(BF16))

        return begin, end

    items = [token_item(late, late_at, wckv, ck, cvext)]
    items += [
        project(first, start)
        for start in range(qwidth, 3 * qwidth, CHUNK)
        for first in range(0, halo, TILE)
    ]
    staggered(items)
    for copy in scalars:
        copy.wait()

    def self_item(pair, f, shifted):
        heads = [2 * pair, 2 * pair + 1]
        lanes = lanes_of(pair)
        inner = blocks - 1 - f
        count = WMAX - inner
        start = pl.multiple_of(local_block(f, odd, blocks) * BLK, BLK)
        first = pl.multiple_of(jnp.where(odd, 0, halo - count * BLK), BLK)
        at = pl.ds(first, count * BLK)

        def begin():
            return pair_scores(q[pl.ds(start, BLK), lanes], keys[at, lanes])

        def end(scores):
            bias = [[] for _ in heads]
            for mine_bias, h in zip(bias, heads):
                width = jnp.where(exists, band[h], 0)
                for t in range(count):
                    one, two = band_bias(width, inner + 1 + t), band_bias(width, inner + count - t)
                    mine_bias.append(jnp.where(odd, one, two))
            scales = [factor[h] * (HD**-0.5 * LOG2E) for h in heads]
            part, weight, shifts = pair_sums(scores, vext[pair, at, :], scales, bias, shifted)
            to = slice((f - done) * BLK, (f - done + 1) * BLK)
            had, had_weight = acc_in[to, lanes], sum_in[to, lanes]
            if shifted:
                low = low_half(BLK)
                lane = lax.broadcasted_iota(jnp.int32, (BLK, LANES), 1)
                olds = [
                    jnp.sum(jnp.where(lane == h, peak_in[to, :], 0.0), axis=1, keepdims=True)
                    for h in heads
                ]
                news = [jnp.maximum(a, b) for a, b in zip(olds, shifts)]
                keep = [jnp.exp2(a - n) for a, n in zip(olds, news)]
                add = [jnp.exp2(b - n) for b, n in zip(shifts, news)]
                keep = jnp.where(low, keep[0], keep[1])
                add = jnp.where(low, add[0], add[1])
                had, had_weight = had * keep, had_weight * keep
                part, weight = part * add, weight * add
            mine[to, lanes] = ((had + part) / (had_weight + weight)).astype(BF16)

        return begin, end

    biases = [
        token_bias(
            align,
            counts,
            local_block(f, odd, blocks),
            device * (tokens // TOKB) - RCH,
            window,
        )
        for f in range(done, blocks)
    ]

    def cross_item(pair, f, shifted):
        lanes = lanes_of(pair)
        start = pl.multiple_of(local_block(f, odd, blocks) * BLK, BLK)

        def begin():
            return pair_scores(cq[pl.ds(start, BLK), lanes], ck[:, lanes])

        def end(scores):
            scales = [temp[2 * pair + i] * (HD**-0.5 * LOG2E) for i in range(2)]
            part, weight, _ = pair_sums(
                scores, cvext[pair], scales, [[biases[f - done]]] * 2, shifted
            )
            to = slice((f - done) * BLK, (f - done + 1) * BLK)
            cross_mine[to, lanes] = (part / weight).astype(BF16)

        return begin, end

    pairs, cross_pairs = qwidth // LANES, cwidth // LANES
    easy = plain(factor, temp)

    @pl.when(easy)
    def _():
        items = [
            cross_item(p, f, False) for p in range(cross_pairs) for f in range(done, blocks)
        ]
        items += [self_item(p, f, False) for p in range(pairs) for f in range(done, blocks)]
        staggered(items, 2)

    @pl.when(jnp.logical_not(easy))
    def _():
        @pl.loop(0, pairs)
        def _(p):
            staggered([self_item(p, f, True) for f in range(done, blocks)])

        @pl.loop(0, cross_pairs)
        def _(p):
            staggered([cross_item(p, f, True) for f in range(done, blocks)])

    total = dot(mine[...], wo[...]) + dot(cross_mine[...], wco[...])
    for copy in finish(total, out, stage, sems, done, WMAX, odd, blocks):
        copy.wait()


def shards(
    frames,
    context,
    noise_level,
    alignment,
    counts,
    band_width,
    mod_table,
    qkv_weight,
    out_weight,
    cross_query_weight,
    cross_kv_weight,
    cross_out_weight,
    banded_attender_factor,
    cross_temp,
):
    rows, width = frames.shape
    blocks = rows // BLK
    halo = WMAX * BLK
    done = blocks - WMAX
    tokens, cwidth = context.shape
    qwidth = qkv_weight.shape[1] // 3
    cqwidth = cross_query_weight.shape[1]
    pairs, cross_pairs = qwidth // LANES, cqwidth // LANES
    window = tokens + 2 * RCH * TOKB
    devices = lax.axis_size("seq")
    vmem = pl.BlockSpec(memory_space=pltpu.VMEM)
    hbm = pl.BlockSpec(memory_space=pltpu.HBM)
    pack_rows = halo + TOK_PACK

    hidden, near, far, context = pl.pallas_call(
        hidden_kernel,
        out_shape=[
            jax.ShapeDtypeStruct((rows, width), BF16),
            jax.ShapeDtypeStruct((pack_rows, width), BF16),
            jax.ShapeDtypeStruct((pack_rows, width), BF16),
            jax.ShapeDtypeStruct(context.shape, BF16),
        ],
        in_specs=[hbm] * 4,
        out_specs=[vmem] * 4,
        scratch_shapes=[
            pltpu.SMEM(noise_level.shape, jnp.int32),
            pltpu.VMEM(mod_table.shape, F32),
            pltpu.VMEM((rows, width), BF16),
            pltpu.SemaphoreType.DMA((blocks + 4,)),
        ],
        compiler_params=pltpu.CompilerParams(vmem_limit_bytes=8 * 2**20),
        cost_estimate=pl.CostEstimate(flops=8 * 10**9, bytes_accessed=4 * 10**6, transcendentals=0),
        name="hidden_and_packs",
    )(*in_hbm(noise_level, frames, mod_table, context))

    same_chip = [(i, i ^ 1) for i in range(devices) if i ^ 1 < devices]
    across = [(i, i + 1) for i in range(1, devices - 1, 2)]
    across += [(b, a) for a, b in across]
    near_got = lax.ppermute(near, "seq", same_chip)
    far_got = lax.ppermute(far, "seq", across)

    open_rows = WMAX * BLK
    scalar_scratch = [
        pltpu.SMEM(band_width.shape, jnp.int32),
        pltpu.SMEM(banded_attender_factor.shape, F32),
        pltpu.SMEM(cross_temp.shape, F32),
        pltpu.SMEM(alignment.shape[::-1], jnp.int32),
        pltpu.SMEM(counts.shape, jnp.int32),
    ]
    scalars = in_hbm(band_width, banded_attender_factor, cross_temp, alignment.T, counts)
    loads = 2
    update, acc, weight, peaks, q, cq, wo, wco, ck, cvext = pl.pallas_call(
        main_kernel,
        out_shape=[
            jax.ShapeDtypeStruct((rows, width), BF16),
            jax.ShapeDtypeStruct((open_rows, qwidth), F32),
            jax.ShapeDtypeStruct((open_rows, qwidth), F32),
            jax.ShapeDtypeStruct((open_rows, LANES), F32),
            jax.ShapeDtypeStruct((rows, qwidth), BF16),
            jax.ShapeDtypeStruct((rows, cqwidth), BF16),
            jax.ShapeDtypeStruct(out_weight.shape, BF16),
            jax.ShapeDtypeStruct(cross_out_weight.shape, BF16),
            jax.ShapeDtypeStruct((window, cqwidth), BF16),
            jax.ShapeDtypeStruct((cross_pairs, window, 2 * LANES), BF16),
        ],
        in_specs=[hbm] * 5 + [vmem] * 6 + [hbm] * 2,
        out_specs=[hbm] + [vmem] * 9,
        scratch_shapes=scalar_scratch
        + [
            pltpu.VMEM((window, cwidth), BF16),
            pltpu.VMEM((rows + halo, qwidth), BF16),
            pltpu.VMEM((pairs, rows + halo, 2 * LANES), BF16),
            pltpu.VMEM((done * BLK, qwidth), BF16),
            pltpu.VMEM((done * BLK, cqwidth), BF16),
            pltpu.VMEM((done * BLK, width), BF16),
            pltpu.SemaphoreType.DMA((loads + 5,)),
        ],
        compiler_params=pltpu.CompilerParams(vmem_limit_bytes=MAIN_VMEM),
        cost_estimate=pl.CostEstimate(
            flops=12 * 10**9, bytes_accessed=20 * 10**6, transcendentals=5 * 10**6
        ),
        name="local_attention",
    )(
        *scalars,
        hidden,
        near_got,
        context,
        qkv_weight,
        cross_query_weight,
        cross_kv_weight,
        *in_hbm(out_weight, cross_out_weight),
    )

    return pl.pallas_call(
        tail_kernel,
        out_shape=jax.ShapeDtypeStruct((rows, width), BF16),
        in_specs=[hbm] * 5 + [vmem] * 12 + [hbm],
        out_specs=hbm,
        scratch_shapes=scalar_scratch
        + [
            pltpu.VMEM((RCH * TOKB, cwidth), BF16),
            pltpu.VMEM((halo, qwidth), BF16),
            pltpu.VMEM((pairs, halo, 2 * LANES), BF16),
            pltpu.VMEM((window, cqwidth), BF16),
            pltpu.VMEM((cross_pairs, window, 2 * LANES), BF16),
            pltpu.VMEM((open_rows, qwidth), BF16),
            pltpu.VMEM((open_rows, cqwidth), BF16),
            pltpu.VMEM((open_rows, width), BF16),
            pltpu.SemaphoreType.DMA((WMAX + 5,)),
        ],
        input_output_aliases={17: 0},
        compiler_params=pltpu.CompilerParams(vmem_limit_bytes=TAIL_VMEM),
        cost_estimate=pl.CostEstimate(
            flops=5 * 10**9, bytes_accessed=12 * 10**6, transcendentals=10**6
        ),
        name="halo_attention",
    )(
        *scalars,
        far_got,
        qkv_weight,
        wo,
        wco,
        cross_kv_weight,
        ck,
        cvext,
        acc,
        weight,
        peaks,
        q,
        cq,
        update,
    )


def solution(mesh):
    placed = (
        P(("groups", "seq"), None),
        P(("groups", "seq"), None),
        P(("groups", "seq")),
        P(("groups", "seq"), None),
        P(("groups", "seq")),
        P(),
        P(),
        P(),
        P(),
        P(),
        P(),
        P(),
        P(),
        P(),
    )
    return jax.shard_map(
        shards, mesh=mesh, in_specs=placed, out_specs=P(("groups", "seq"), None), check_vma=False
    )
```

```python
import jax
import jax.numpy as jnp
from jax import lax
from jax.experimental import pallas as pl
from jax.experimental.pallas import tpu as pltpu
from jax.sharding import PartitionSpec as P

BANDED_ATTEND_CT = 16
MIXED_ATTEND_CNT = 8
HD = 64
LEVELS = 8
BLK = 128
WMAX = 2
TOKB = 48
RCH = 1
ALIST = 2

LANES = 128
CHUNK = 512
TILE = 256
LOG2E = 1.4426950408889634
OFF = -1e30
PLAIN_FACTOR = 8.0
F32 = jnp.float32
BF16 = jnp.bfloat16
MAIN_VMEM = 24 * 2**20
TAIL_VMEM = 16 * 2**20
TOK_PACK = 32


def dot(a, b):
    return jnp.dot(a, b, preferred_element_type=F32)


def dot_t(a, b):
    return lax.dot_general(a, b, (((1,), (1,)), ((), ())), preferred_element_type=F32)


def low_half(rows):
    return lax.broadcasted_iota(jnp.int32, (rows, LANES), 1) < HD


def head_norm(x):
    low = low_half(x.shape[0])
    done = []
    for start in range(0, x.shape[1], LANES):
        pair = x[:, start : start + LANES]
        square = pair * pair
        first = jnp.sum(jnp.where(low, square, 0.0), axis=1, keepdims=True)
        second = jnp.sum(jnp.where(low, 0.0, square), axis=1, keepdims=True)
        mean = jnp.where(low, first, second) * (1.0 / HD)
        done.append((pair * lax.rsqrt(mean + 1e-06)).astype(BF16))
    return jnp.concatenate(done, 1)


def staggered(items, delay=1):
    begun = []
    for begin, end in items:
        begun.append((end, begin()))
        if len(begun) > delay:
            end, value = begun.pop(0)
            end(value)
    for end, value in begun:
        end(value)


def pair_scores(q, k):
    low = low_half(q.shape[0])
    zero = jnp.zeros_like(q)
    stacked = jnp.concatenate([jnp.where(low, q, zero), jnp.where(low, zero, q)], 0)
    return dot_t(stacked, k)


def pair_sums(scores, vext, scales, tile_bias, shifted):
    rows = scores.shape[0] // 2
    parts, shifts = [], []
    for head in range(2):
        mine = scores[head * rows : (head + 1) * rows]
        biases = tile_bias[head]
        width = mine.shape[1] // len(biases)
        tiles = []
        for t, bias in enumerate(biases):
            tile = mine[:, t * width : (t + 1) * width] * scales[head]
            tiles.append(tile if bias is None else tile + bias)
        if shifted:
            peak = tiles[0]
            for tile in tiles[1:]:
                peak = jnp.maximum(peak, tile)
            peak = jnp.max(peak, axis=1, keepdims=True)
            shifts.append(peak)
            tiles = [tile - peak for tile in tiles]
        tiles = [jnp.exp2(tile).astype(BF16) for tile in tiles]
        parts.append(tiles[0] if len(tiles) == 1 else jnp.concatenate(tiles, 1))
    got = dot(jnp.concatenate(parts, 0), vext)
    low = low_half(rows)
    total = jnp.where(low, got[:rows, :LANES], got[rows:, :LANES])
    weight = jnp.where(low, got[:rows, LANES:], got[rows:, LANES:])
    return total, weight, shifts


def band_bias(width, distance):
    return jnp.where(width >= distance, 0.0, OFF).astype(F32)


def plain(factor, temp):
    flag = factor[0] <= PLAIN_FACTOR
    for i in range(1, BANDED_ATTEND_CT):
        flag = flag & (factor[i] <= PLAIN_FACTOR)
    for i in range(MIXED_ATTEND_CNT):
        flag = flag & (temp[i] <= PLAIN_FACTOR)
    return flag


def token_bias(align, counts, block, first_token_block, window):
    place = lax.broadcasted_iota(jnp.int32, (1, window), 1) // TOKB + first_token_block
    allowed = place == align[0, block]
    for slot in range(1, ALIST):
        live = jnp.where(slot < counts[block], align[slot, block], -RCH - 1)
        allowed = allowed | (place == live)
    return jnp.where(allowed, 0.0, OFF).astype(F32)


def local_block(f, odd, blocks):
    return jnp.where(odd, f, blocks - 1 - f)


def in_hbm(*arrays):
    return [pltpu.with_memory_space_constraint(a, pltpu.HBM) for a in arrays]


def lanes_of(pair):
    if isinstance(pair, int):
        return slice(pair * LANES, (pair + 1) * LANES)
    return pl.ds(pl.multiple_of(pair * LANES, LANES), LANES)


def hidden_kernel(
    level_in,
    frames,
    table_in,
    context_in,
    hidden,
    near,
    far,
    context,
    level,
    table,
    stage,
    sems,
):
    odd = lax.rem(lax.axis_index("seq"), 2) == 1
    rows, width = frames.shape
    blocks = rows // BLK
    loads = [(level_in, level), (table_in, table)]
    loads += [
        (frames.at[pl.ds(b * BLK, BLK)], stage.at[pl.ds(b * BLK, BLK)]) for b in range(blocks)
    ]
    loads.append((context_in, context))
    loads = [pltpu.make_async_copy(a, b, sems.at[i]) for i, (a, b) in enumerate(loads)]
    for load in loads:
        load.start()
    loads[0].wait()
    loads[1].wait()
    for b in range(blocks):
        at = pl.ds(b * BLK, BLK)
        row = table[pl.ds(level[b], 1), :]
        loads[2 + b].wait()
        x = stage[at, :].astype(F32)
        x = x * lax.rsqrt(jnp.mean(x * x, axis=1, keepdims=True) + 1e-06)
        hidden[at, :] = (x * (1.0 + row[:, :width]) + row[:, width:]).astype(BF16)
    loads[2 + blocks].wait()
    halo = WMAX * BLK
    tokens = context.shape[0]
    cwidth = context.shape[1]
    for pack, high in ((near, jnp.logical_not(odd)), (far, odd)):
        start = pl.multiple_of(jnp.where(high, rows - halo, 0), BLK)
        pack[:halo, :] = hidden[pl.ds(start, halo), :]
        start = pl.multiple_of(jnp.where(high, tokens - RCH * TOKB, 0), 16)
        tok = context[pl.ds(start, RCH * TOKB), :]
        pack[halo:, :cwidth] = tok[:TOK_PACK]
        pack[halo : halo + 16, cwidth:] = tok[TOK_PACK:]
        pack[halo + 16 :, cwidth:] = jnp.zeros((TOK_PACK - 16, cwidth), BF16)
    for load in loads[3 + blocks :]:
        load.wait()


def unpack_tokens(pack, halo, cwidth):
    return jnp.concatenate(
        [pack[halo : halo + TOK_PACK, :cwidth], pack[halo : halo + 16, cwidth:]], 0
    )


def token_item(rows, start, wckv, ck, cvext):
    at = pl.ds(start, rows.shape[0])
    cwidth = ck.shape[1]

    def begin():
        return dot(rows[...], wckv[...])

    def end(x):
        ck[at, :] = head_norm(x[:, :cwidth])
        store_values(cvext, at, 0, x[:, cwidth:].astype(BF16))

    return begin, end


def store_values(vext, at, start, values):
    for i in range(values.shape[1] // LANES):
        vext[start // LANES + i, at, :LANES] = values[:, lanes_of(i)]


def scalar_copies(sources, targets, sems, first):
    copies = []
    for i, (source, target) in enumerate(zip(sources, targets)):
        copies.append(pltpu.make_async_copy(source, target, sems.at[first + i]))
        copies[-1].start()
    return copies


def finish(total, out, stage, sems, first, count, odd, blocks):
    copies = []
    for i in range(count):
        at = pl.ds(i * BLK, BLK)
        stage[at, :] = total[i * BLK : (i + 1) * BLK].astype(BF16)
        to = pl.multiple_of(local_block(first + i, odd, blocks) * BLK, BLK)
        copies.append(
            pltpu.make_async_copy(stage.at[at], out.at[pl.ds(to, BLK)], sems.at[i])
        )
        copies[-1].start()
    return copies


def main_kernel(
    band_in,
    factor_in,
    temp_in,
    align_in,
    counts_in,
    hidden,
    near,
    context,
    wqkv,
    wcq,
    wckv,
    wo_in,
    wco_in,
    out,
    acc_out,
    sum_out,
    peak_out,
    q,
    cq,
    wo,
    wco,
    ck,
    cvext,
    band,
    factor,
    temp,
    align,
    counts,
    tokens,
    keys,
    vext,
    mine,
    cross_mine,
    stage,
    sems,
):
    device = lax.axis_index("seq")
    odd = lax.rem(device, 2) == 1
    rows = hidden.shape[0]
    blocks = rows // BLK
    halo = WMAX * BLK
    done = blocks - WMAX
    qwidth = q.shape[1]
    cwidth = context.shape[1]
    own = jnp.where(odd, halo, 0)
    other = jnp.where(odd, 0, rows)

    loads = [(wo_in, wo), (wco_in, wco)]
    loads = [pltpu.make_async_copy(a, b, sems.at[i]) for i, (a, b) in enumerate(loads)]
    scalars = scalar_copies(
        (band_in, factor_in, temp_in, align_in, counts_in),
        (band, factor, temp, align, counts),
        sems,
        len(loads),
    )
    for load in loads:
        load.start()

    vext[:, :, LANES:] = jnp.ones((vext.shape[0], vext.shape[1], LANES), BF16)
    cvext[:, :, LANES:] = jnp.ones((cvext.shape[0], cvext.shape[1], LANES), BF16)
    tokens[...] = jnp.zeros_like(tokens)
    tokens[RCH * TOKB : RCH * TOKB + context.shape[0], :] = context[...]
    start = jnp.where(odd, 0, RCH * TOKB + context.shape[0])
    tokens[pl.ds(pl.multiple_of(start, 16), RCH * TOKB), :] = unpack_tokens(near, halo, cwidth)

    def project(source, first, to, start):
        def begin():
            return dot(source[first : first + TILE, :], wqkv[:, start : start + CHUNK])

        def end(x):
            at = pl.ds(pl.multiple_of(to + first, BLK), TILE)
            part, col = divmod(start, qwidth)
            if part == 0:
                q[first : first + TILE, col : col + CHUNK] = head_norm(x)
            elif part == 1:
                keys[at, col : col + CHUNK] = head_norm(x)
            else:
                store_values(vext, at, col, x.astype(BF16))

        return begin, end

    def project_cross(first):
        def begin():
            return dot(hidden[first : first + TILE, :], wcq[...])

        def end(x):
            cq[first : first + TILE, :] = head_norm(x)

        return begin, end

    items = []
    for start in range(0, 3 * qwidth, CHUNK):
        tiles = [project(hidden, first, own, start) for first in range(0, rows, TILE)]
        if start >= qwidth:
            tiles += [project(near, first, other, start) for first in range(0, halo, TILE)]
        items += tiles
    items += [project_cross(first) for first in range(0, rows, TILE)]
    items.append(token_item(tokens, 0, wckv, ck, cvext))
    staggered(items)
    for copy in scalars:
        copy.wait()

    def self_item(pair, f, shifted):
        heads = [2 * pair, 2 * pair + 1]
        lanes = lanes_of(pair)
        inner = min(WMAX, blocks - 1 - f)
        count = WMAX + 1 + inner
        start = pl.multiple_of(local_block(f, odd, blocks) * BLK, BLK)
        first = pl.multiple_of(jnp.where(odd, f, blocks - 1 - f - inner) * BLK, BLK)
        at = pl.ds(first, count * BLK)

        def begin():
            return pair_scores(q[pl.ds(start, BLK), lanes], keys[at, lanes])

        def end(scores):
            bias = [[] for _ in heads]
            for mine_bias, h in zip(bias, heads):
                by_distance = [0.0] + [band_bias(band[h], d) for d in range(1, WMAX + 1)]
                for t in range(count):
                    one, two = abs(t - WMAX), abs(t - inner)
                    if one == two:
                        mine_bias.append(None if one == 0 else by_distance[one])
                    else:
                        mine_bias.append(jnp.where(odd, by_distance[one], by_distance[two]))
            scales = [factor[h] * (HD**-0.5 * LOG2E) for h in heads]
            part, weight, shifts = pair_sums(scores, vext[pair, at, :], scales, bias, shifted)
            if f < done:
                mine[f * BLK : (f + 1) * BLK, lanes] = (part / weight).astype(BF16)
                return
            to = slice((f - done) * BLK, (f - done + 1) * BLK)
            acc_out[to, lanes] = part
            sum_out[to, lanes] = weight
            if shifted:
                lane = lax.broadcasted_iota(jnp.int32, (BLK, LANES), 1)
                peaks = peak_out[to, :]
                for h, shift in zip(heads, shifts):
                    peaks = jnp.where(lane == h, shift, peaks)
                peak_out[to, :] = peaks

        return begin, end

    biases = [
        token_bias(
            align,
            counts,
            local_block(f, odd, blocks),
            device * (context.shape[0] // TOKB) - RCH,
            tokens.shape[0],
        )
        for f in range(done)
    ]

    def cross_item(pair, f, shifted):
        lanes = lanes_of(pair)
        start = pl.multiple_of(local_block(f, odd, blocks) * BLK, BLK)

        def begin():
            return pair_scores(cq[pl.ds(start, BLK), lanes], ck[:, lanes])

        def end(scores):
            scales = [temp[2 * pair + i] * (HD**-0.5 * LOG2E) for i in range(2)]
            part, weight, _ = pair_sums(
                scores, cvext[pair], scales, [[biases[f]]] * 2, shifted
            )
            cross_mine[f * BLK : (f + 1) * BLK, lanes] = (part / weight).astype(BF16)

        return begin, end

    pairs, cross_pairs = qwidth // LANES, cwidth // LANES
    easy = plain(factor, temp)

    def project_out():
        for load in loads:
            load.wait()
        total = dot(mine[...], wo[...]) + dot(cross_mine[...], wco[...])
        return finish(total, out, stage, sems, 0, done, odd, blocks)

    @pl.when(easy)
    def _():
        items = [cross_item(p, f, False) for p in range(cross_pairs) for f in range(done)]
        items += [self_item(p, f, False) for p in range(pairs) for f in range(done)]
        staggered(items, 2)
        copies = project_out()
        staggered(
            [self_item(p, f, False) for p in range(pairs) for f in range(done, blocks)], 2
        )
        for copy in copies:
            copy.wait()

    @pl.when(jnp.logical_not(easy))
    def _():
        peak_out[...] = jnp.zeros_like(peak_out)

        @pl.loop(0, pairs)
        def _(p):
            staggered([self_item(p, f, True) for f in range(blocks)])

        @pl.loop(0, cross_pairs)
        def _(p):
            staggered([cross_item(p, f, True) for f in range(done)])

        for copy in project_out():
            copy.wait()


def tail_kernel(
    band_in,
    factor_in,
    temp_in,
    align_in,
    counts_in,
    pack,
    wqkv,
    wo,
    wco,
    wckv,
    ck_in,
    cvext_in,
    acc_in,
    sum_in,
    peak_in,
    q,
    cq,
    partial_out,
    out,
    band,
    factor,
    temp,
    align,
    counts,
    late,
    keys,
    vext,
    ck,
    cvext,
    mine,
    cross_mine,
    stage,
    sems,
):
    device = lax.axis_index("seq")
    odd = lax.rem(device, 2) == 1
    last = lax.axis_size("seq") - 1
    exists = jnp.where(odd, device < last, device > 0)
    rows, qwidth = q.shape
    blocks = rows // BLK
    halo = WMAX * BLK
    done = blocks - WMAX
    window, cwidth = ck.shape
    tokens = window - 2 * RCH * TOKB

    scalars = scalar_copies(
        (band_in, factor_in, temp_in, align_in, counts_in),
        (band, factor, temp, align, counts),
        sems,
        0,
    )
    vext[:, :, LANES:] = jnp.ones((vext.shape[0], vext.shape[1], LANES), BF16)
    ck[...] = ck_in[...]
    cvext[...] = cvext_in[...]
    late[...] = unpack_tokens(pack, halo, wckv.shape[0])
    late_at = pl.multiple_of(jnp.where(odd, window - RCH * TOKB, 0), 16)

    def project(first, start):
        def begin():
            return dot(pack[first : first + TILE, :], wqkv[:, start : start + CHUNK])

        def end(x):
            part, col = divmod(start, qwidth)
            at = slice(first, first + TILE)
            if part == 1:
                keys[at, col : col + CHUNK] = head_norm(x)
            else:
                store_values(vext, at, col, x.astype(BF16))

        return begin, end

    items = [token_item(late, late_at, wckv, ck, cvext)]
    items += [
        project(first, start)
        for start in range(qwidth, 3 * qwidth, CHUNK)
        for first in range(0, halo, TILE)
    ]
    staggered(items)
    for copy in scalars:
        copy.wait()

    def self_item(pair, f, shifted):
        heads = [2 * pair, 2 * pair + 1]
        lanes = lanes_of(pair)
        inner = blocks - 1 - f
        count = WMAX - inner
        start = pl.multiple_of(local_block(f, odd, blocks) * BLK, BLK)
        first = pl.multiple_of(jnp.where(odd, 0, halo - count * BLK), BLK)
        at = pl.ds(first, count * BLK)

        def begin():
            return pair_scores(q[pl.ds(start, BLK), lanes], keys[at, lanes])

        def end(scores):
            bias = [[] for _ in heads]
            for mine_bias, h in zip(bias, heads):
                width = jnp.where(exists, band[h], 0)
                for t in range(count):
                    one, two = band_bias(width, inner + 1 + t), band_bias(width, inner + count - t)
                    mine_bias.append(jnp.where(odd, one, two))
            scales = [factor[h] * (HD**-0.5 * LOG2E) for h in heads]
            part, weight, shifts = pair_sums(scores, vext[pair, at, :], scales, bias, shifted)
            to = slice((f - done) * BLK, (f - done + 1) * BLK)
            had, had_weight = acc_in[to, lanes], sum_in[to, lanes]
            if shifted:
                low = low_half(BLK)
                lane = lax.broadcasted_iota(jnp.int32, (BLK, LANES), 1)
                olds = [
                    jnp.sum(jnp.where(lane == h, peak_in[to, :], 0.0), axis=1, keepdims=True)
                    for h in heads
                ]
                news = [jnp.maximum(a, b) for a, b in zip(olds, shifts)]
                keep = [jnp.exp2(a - n) for a, n in zip(olds, news)]
                add = [jnp.exp2(b - n) for b, n in zip(shifts, news)]
                keep = jnp.where(low, keep[0], keep[1])
                add = jnp.where(low, add[0], add[1])
                had, had_weight = had * keep, had_weight * keep
                part, weight = part * add, weight * add
            mine[to, lanes] = ((had + part) / (had_weight + weight)).astype(BF16)

        return begin, end

    biases = [
        token_bias(
            align,
            counts,
            local_block(f, odd, blocks),
            device * (tokens // TOKB) - RCH,
            window,
        )
        for f in range(done, blocks)
    ]

    def cross_item(pair, f, shifted):
        lanes = lanes_of(pair)
        start = pl.multiple_of(local_block(f, odd, blocks) * BLK, BLK)

        def begin():
            return pair_scores(cq[pl.ds(start, BLK), lanes], ck[:, lanes])

        def end(scores):
            scales = [temp[2 * pair + i] * (HD**-0.5 * LOG2E) for i in range(2)]
            part, weight, _ = pair_sums(
                scores, cvext[pair], scales, [[biases[f - done]]] * 2, shifted
            )
            to = slice((f - done) * BLK, (f - done + 1) * BLK)
            cross_mine[to, lanes] = (part / weight).astype(BF16)

        return begin, end

    pairs, cross_pairs = qwidth // LANES, cwidth // LANES
    easy = plain(factor, temp)

    @pl.when(easy)
    def _():
        items = [
            cross_item(p, f, False) for p in range(cross_pairs) for f in range(done, blocks)
        ]
        items += [self_item(p, f, False) for p in range(pairs) for f in range(done, blocks)]
        staggered(items, 3)

    @pl.when(jnp.logical_not(easy))
    def _():
        @pl.loop(0, pairs)
        def _(p):
            staggered([self_item(p, f, True) for f in range(done, blocks)])

        @pl.loop(0, cross_pairs)
        def _(p):
            staggered([cross_item(p, f, True) for f in range(done, blocks)])

    copies = []
    for start in range(0, wo.shape[1], CHUNK):
        cols = slice(start, start + CHUNK)
        total = dot(mine[...], wo[:, cols]) + dot(cross_mine[...], wco[:, cols])
        stage[:, cols] = total.astype(BF16)
        for i in range(WMAX):
            to = pl.multiple_of(local_block(done + i, odd, blocks) * BLK, BLK)
            copies.append(
                pltpu.make_async_copy(
                    stage.at[pl.ds(i * BLK, BLK), pl.ds(start, CHUNK)],
                    out.at[pl.ds(to, BLK), pl.ds(start, CHUNK)],
                    sems.at[len(copies)],
                )
            )
            copies[-1].start()
    for copy in copies:
        copy.wait()


def shards(
    frames,
    context,
    noise_level,
    alignment,
    counts,
    band_width,
    mod_table,
    qkv_weight,
    out_weight,
    cross_query_weight,
    cross_kv_weight,
    cross_out_weight,
    banded_attender_factor,
    cross_temp,
):
    rows, width = frames.shape
    blocks = rows // BLK
    halo = WMAX * BLK
    done = blocks - WMAX
    tokens, cwidth = context.shape
    qwidth = qkv_weight.shape[1] // 3
    cqwidth = cross_query_weight.shape[1]
    pairs, cross_pairs = qwidth // LANES, cqwidth // LANES
    window = tokens + 2 * RCH * TOKB
    devices = lax.axis_size("seq")
    vmem = pl.BlockSpec(memory_space=pltpu.VMEM)
    hbm = pl.BlockSpec(memory_space=pltpu.HBM)
    pack_rows = halo + TOK_PACK

    hidden, near, far, context = pl.pallas_call(
        hidden_kernel,
        out_shape=[
            jax.ShapeDtypeStruct((rows, width), BF16),
            jax.ShapeDtypeStruct((pack_rows, width), BF16),
            jax.ShapeDtypeStruct((pack_rows, width), BF16),
            jax.ShapeDtypeStruct(context.shape, BF16),
        ],
        in_specs=[hbm] * 4,
        out_specs=[vmem] * 4,
        scratch_shapes=[
            pltpu.SMEM(noise_level.shape, jnp.int32),
            pltpu.VMEM(mod_table.shape, F32),
            pltpu.VMEM((rows, width), BF16),
            pltpu.SemaphoreType.DMA((blocks + 4,)),
        ],
        compiler_params=pltpu.CompilerParams(vmem_limit_bytes=8 * 2**20),
        cost_estimate=pl.CostEstimate(flops=8 * 10**9, bytes_accessed=4 * 10**6, transcendentals=0),
        name="hidden_and_packs",
    )(*in_hbm(noise_level, frames, mod_table, context))

    same_chip = [(i, i ^ 1) for i in range(devices) if i ^ 1 < devices]
    across = [(i, i + 1) for i in range(1, devices - 1, 2)]
    across += [(b, a) for a, b in across]
    near_got = lax.ppermute(near, "seq", same_chip)
    far_got = lax.ppermute(far, "seq", across)

    open_rows = WMAX * BLK
    scalar_scratch = [
        pltpu.SMEM(band_width.shape, jnp.int32),
        pltpu.SMEM(banded_attender_factor.shape, F32),
        pltpu.SMEM(cross_temp.shape, F32),
        pltpu.SMEM(alignment.shape[::-1], jnp.int32),
        pltpu.SMEM(counts.shape, jnp.int32),
    ]
    scalars = in_hbm(band_width, banded_attender_factor, cross_temp, alignment.T, counts)
    loads = 2
    update, acc, weight, peaks, q, cq, wo, wco, ck, cvext = pl.pallas_call(
        main_kernel,
        out_shape=[
            jax.ShapeDtypeStruct((rows, width), BF16),
            jax.ShapeDtypeStruct((open_rows, qwidth), F32),
            jax.ShapeDtypeStruct((open_rows, qwidth), F32),
            jax.ShapeDtypeStruct((open_rows, LANES), F32),
            jax.ShapeDtypeStruct((rows, qwidth), BF16),
            jax.ShapeDtypeStruct((rows, cqwidth), BF16),
            jax.ShapeDtypeStruct(out_weight.shape, BF16),
            jax.ShapeDtypeStruct(cross_out_weight.shape, BF16),
            jax.ShapeDtypeStruct((window, cqwidth), BF16),
            jax.ShapeDtypeStruct((cross_pairs, window, 2 * LANES), BF16),
        ],
        in_specs=[hbm] * 5 + [vmem] * 6 + [hbm] * 2,
        out_specs=[hbm] + [vmem] * 9,
        scratch_shapes=scalar_scratch
        + [
            pltpu.VMEM((window, cwidth), BF16),
            pltpu.VMEM((rows + halo, qwidth), BF16),
            pltpu.VMEM((pairs, rows + halo, 2 * LANES), BF16),
            pltpu.VMEM((done * BLK, qwidth), BF16),
            pltpu.VMEM((done * BLK, cqwidth), BF16),
            pltpu.VMEM((done * BLK, width), BF16),
            pltpu.SemaphoreType.DMA((loads + 5,)),
        ],
        compiler_params=pltpu.CompilerParams(vmem_limit_bytes=MAIN_VMEM),
        cost_estimate=pl.CostEstimate(
            flops=12 * 10**9, bytes_accessed=20 * 10**6, transcendentals=5 * 10**6
        ),
        name="local_attention",
    )(
        *scalars,
        hidden,
        near_got,
        context,
        qkv_weight,
        cross_query_weight,
        cross_kv_weight,
        *in_hbm(out_weight, cross_out_weight),
    )

    return pl.pallas_call(
        tail_kernel,
        out_shape=jax.ShapeDtypeStruct((rows, width), BF16),
        in_specs=[hbm] * 5 + [vmem] * 12 + [hbm],
        out_specs=hbm,
        scratch_shapes=scalar_scratch
        + [
            pltpu.VMEM((RCH * TOKB, cwidth), BF16),
            pltpu.VMEM((halo, qwidth), BF16),
            pltpu.VMEM((pairs, halo, 2 * LANES), BF16),
            pltpu.VMEM((window, cqwidth), BF16),
            pltpu.VMEM((cross_pairs, window, 2 * LANES), BF16),
            pltpu.VMEM((open_rows, qwidth), BF16),
            pltpu.VMEM((open_rows, cqwidth), BF16),
            pltpu.VMEM((open_rows, width), BF16),
            pltpu.SemaphoreType.DMA((max(5, WMAX * width // CHUNK),)),
        ],
        input_output_aliases={17: 0},
        compiler_params=pltpu.CompilerParams(vmem_limit_bytes=TAIL_VMEM),
        cost_estimate=pl.CostEstimate(
            flops=5 * 10**9, bytes_accessed=12 * 10**6, transcendentals=10**6
        ),
        name="halo_attention",
    )(
        *scalars,
        far_got,
        qkv_weight,
        wo,
        wco,
        cross_kv_weight,
        ck,
        cvext,
        acc,
        weight,
        peaks,
        q,
        cq,
        update,
    )


def solution(mesh):
    placed = (
        P(("groups", "seq"), None),
        P(("groups", "seq"), None),
        P(("groups", "seq")),
        P(("groups", "seq"), None),
        P(("groups", "seq")),
        P(),
        P(),
        P(),
        P(),
        P(),
        P(),
        P(),
        P(),
        P(),
    )
    return jax.shard_map(
        shards, mesh=mesh, in_specs=placed, out_specs=P(("groups", "seq"), None), check_vma=False
    )
```

```python
import jax
import jax.numpy as jnp
from jax import lax
from jax.experimental import pallas as pl
from jax.experimental.pallas import tpu as pltpu
from jax.sharding import PartitionSpec as P

BANDED_ATTEND_CT = 16
MIXED_ATTEND_CNT = 8
HD = 64
LEVELS = 8
BLK = 128
WMAX = 2
TOKB = 48
RCH = 1
ALIST = 2

LANES = 128
CHUNK = 512
TILE = 256
LOG2E = 1.4426950408889634
OFF = -1e30
PLAIN_FACTOR = 8.0
F32 = jnp.float32
BF16 = jnp.bfloat16
MAIN_VMEM = 24 * 2**20
TAIL_VMEM = 16 * 2**20
TOK_PACK = 32


def dot(a, b):
    return jnp.dot(a, b, preferred_element_type=F32)


def dot_t(a, b):
    return lax.dot_general(a, b, (((1,), (1,)), ((), ())), preferred_element_type=F32)


def low_half(rows):
    return lax.broadcasted_iota(jnp.int32, (rows, LANES), 1) < HD


def head_norm(x):
    low = low_half(x.shape[0])
    done = []
    for start in range(0, x.shape[1], LANES):
        pair = x[:, start : start + LANES]
        square = pair * pair
        first = jnp.sum(jnp.where(low, square, 0.0), axis=1, keepdims=True)
        second = jnp.sum(jnp.where(low, 0.0, square), axis=1, keepdims=True)
        mean = jnp.where(low, first, second) * (1.0 / HD)
        done.append((pair * lax.rsqrt(mean + 1e-06)).astype(BF16))
    return jnp.concatenate(done, 1)


def staggered(items, delay=1):
    begun = []
    for begin, end in items:
        begun.append((end, begin()))
        if len(begun) > delay:
            end, value = begun.pop(0)
            end(value)
    for end, value in begun:
        end(value)


def pair_scores(q, k):
    low = low_half(q.shape[0])
    zero = jnp.zeros_like(q)
    stacked = jnp.concatenate([jnp.where(low, q, zero), jnp.where(low, zero, q)], 0)
    return dot_t(stacked, k)


def pair_sums(scores, vext, scales, tile_bias, shifted):
    rows = scores.shape[0] // 2
    parts, shifts = [], []
    for head in range(2):
        mine = scores[head * rows : (head + 1) * rows]
        biases = tile_bias[head]
        width = mine.shape[1] // len(biases)
        tiles = []
        for t, bias in enumerate(biases):
            tile = mine[:, t * width : (t + 1) * width] * scales[head]
            tiles.append(tile if bias is None else tile + bias)
        if shifted:
            peak = tiles[0]
            for tile in tiles[1:]:
                peak = jnp.maximum(peak, tile)
            peak = jnp.max(peak, axis=1, keepdims=True)
            shifts.append(peak)
            tiles = [tile - peak for tile in tiles]
        tiles = [jnp.exp2(tile).astype(BF16) for tile in tiles]
        parts.append(tiles[0] if len(tiles) == 1 else jnp.concatenate(tiles, 1))
    got = dot(jnp.concatenate(parts, 0), vext)
    low = low_half(rows)
    total = jnp.where(low, got[:rows, :LANES], got[rows:, :LANES])
    weight = jnp.where(low, got[:rows, LANES:], got[rows:, LANES:])
    return total, weight, shifts


def band_bias(width, distance):
    return jnp.where(width >= distance, 0.0, OFF).astype(F32)


def plain(factor, temp):
    flag = factor[0] <= PLAIN_FACTOR
    for i in range(1, BANDED_ATTEND_CT):
        flag = flag & (factor[i] <= PLAIN_FACTOR)
    for i in range(MIXED_ATTEND_CNT):
        flag = flag & (temp[i] <= PLAIN_FACTOR)
    return flag


def token_bias(align, counts, block, first_token_block, window):
    place = lax.broadcasted_iota(jnp.int32, (1, window), 1) // TOKB + first_token_block
    allowed = place == align[0, block]
    for slot in range(1, ALIST):
        live = jnp.where(slot < counts[block], align[slot, block], -RCH - 1)
        allowed = allowed | (place == live)
    return jnp.where(allowed, 0.0, OFF).astype(F32)


def local_block(f, odd, blocks):
    return jnp.where(odd, f, blocks - 1 - f)


def in_hbm(*arrays):
    return [pltpu.with_memory_space_constraint(a, pltpu.HBM) for a in arrays]


def lanes_of(pair):
    if isinstance(pair, int):
        return slice(pair * LANES, (pair + 1) * LANES)
    return pl.ds(pl.multiple_of(pair * LANES, LANES), LANES)


def hidden_kernel(
    level_in,
    frames,
    table_in,
    context_in,
    hidden,
    near,
    far,
    context,
    level,
    table,
    stage,
    sems,
):
    odd = lax.rem(lax.axis_index("seq"), 2) == 1
    rows, width = frames.shape
    blocks = rows // BLK
    loads = [(level_in, level), (table_in, table)]
    loads += [
        (frames.at[pl.ds(b * BLK, BLK)], stage.at[pl.ds(b * BLK, BLK)]) for b in range(blocks)
    ]
    loads.append((context_in, context))
    loads = [pltpu.make_async_copy(a, b, sems.at[i]) for i, (a, b) in enumerate(loads)]
    for load in loads:
        load.start()
    loads[0].wait()
    loads[1].wait()
    for b in range(blocks):
        at = pl.ds(b * BLK, BLK)
        row = table[pl.ds(level[b], 1), :]
        loads[2 + b].wait()
        x = stage[at, :].astype(F32)
        x = x * lax.rsqrt(jnp.mean(x * x, axis=1, keepdims=True) + 1e-06)
        hidden[at, :] = (x * (1.0 + row[:, :width]) + row[:, width:]).astype(BF16)
    loads[2 + blocks].wait()
    halo = WMAX * BLK
    tokens = context.shape[0]
    cwidth = context.shape[1]
    for pack, high in ((near, jnp.logical_not(odd)), (far, odd)):
        start = pl.multiple_of(jnp.where(high, rows - halo, 0), BLK)
        pack[:halo, :] = hidden[pl.ds(start, halo), :]
        start = pl.multiple_of(jnp.where(high, tokens - RCH * TOKB, 0), 16)
        tok = context[pl.ds(start, RCH * TOKB), :]
        pack[halo:, :cwidth] = tok[:TOK_PACK]
        pack[halo : halo + 16, cwidth:] = tok[TOK_PACK:]
        pack[halo + 16 :, cwidth:] = jnp.zeros((TOK_PACK - 16, cwidth), BF16)
    for load in loads[3 + blocks :]:
        load.wait()


def unpack_tokens(pack, halo, cwidth):
    return jnp.concatenate(
        [pack[halo : halo + TOK_PACK, :cwidth], pack[halo : halo + 16, cwidth:]], 0
    )


def token_item(rows, start, wckv, ck, cvext):
    at = pl.ds(start, rows.shape[0])
    cwidth = ck.shape[1]

    def begin():
        return dot(rows[...], wckv[...])

    def end(x):
        ck[at, :] = head_norm(x[:, :cwidth])
        store_values(cvext, at, 0, x[:, cwidth:].astype(BF16))

    return begin, end


def store_values(vext, at, start, values):
    for i in range(values.shape[1] // LANES):
        vext[start // LANES + i, at, :LANES] = values[:, lanes_of(i)]


def scalar_copies(sources, targets, sems, first):
    copies = []
    for i, (source, target) in enumerate(zip(sources, targets)):
        copies.append(pltpu.make_async_copy(source, target, sems.at[first + i]))
        copies[-1].start()
    return copies


def finish(total, out, stage, sems, first, count, odd, blocks):
    copies = []
    for i in range(count):
        at = pl.ds(i * BLK, BLK)
        stage[at, :] = total[i * BLK : (i + 1) * BLK].astype(BF16)
        to = pl.multiple_of(local_block(first + i, odd, blocks) * BLK, BLK)
        copies.append(
            pltpu.make_async_copy(stage.at[at], out.at[pl.ds(to, BLK)], sems.at[i])
        )
        copies[-1].start()
    return copies


def main_kernel(
    band_in,
    factor_in,
    temp_in,
    align_in,
    counts_in,
    hidden,
    near,
    context,
    wqkv,
    wcq,
    wckv,
    wo_in,
    wco_in,
    out,
    acc_out,
    sum_out,
    peak_out,
    q,
    cq,
    wo,
    wco,
    ck,
    cvext,
    band,
    factor,
    temp,
    align,
    counts,
    tokens,
    keys,
    vext,
    mine,
    cross_mine,
    stage,
    sems,
):
    device = lax.axis_index("seq")
    odd = lax.rem(device, 2) == 1
    rows = hidden.shape[0]
    blocks = rows // BLK
    halo = WMAX * BLK
    done = blocks - WMAX
    qwidth = q.shape[1]
    cwidth = context.shape[1]
    own = jnp.where(odd, halo, 0)
    other = jnp.where(odd, 0, rows)

    loads = [(wo_in, wo), (wco_in, wco)]
    loads = [pltpu.make_async_copy(a, b, sems.at[i]) for i, (a, b) in enumerate(loads)]
    scalars = scalar_copies(
        (band_in, factor_in, temp_in, align_in, counts_in),
        (band, factor, temp, align, counts),
        sems,
        len(loads),
    )
    for load in loads:
        load.start()

    vext[:, :, LANES:] = jnp.ones((vext.shape[0], vext.shape[1], LANES), BF16)
    cvext[:, :, LANES:] = jnp.ones((cvext.shape[0], cvext.shape[1], LANES), BF16)
    tokens[...] = jnp.zeros_like(tokens)
    tokens[RCH * TOKB : RCH * TOKB + context.shape[0], :] = context[...]
    start = jnp.where(odd, 0, RCH * TOKB + context.shape[0])
    tokens[pl.ds(pl.multiple_of(start, 16), RCH * TOKB), :] = unpack_tokens(near, halo, cwidth)

    def project(source, first, to, start):
        def begin():
            return dot(source[first : first + TILE, :], wqkv[:, start : start + CHUNK])

        def end(x):
            at = pl.ds(pl.multiple_of(to + first, BLK), TILE)
            part, col = divmod(start, qwidth)
            if part == 0:
                q[first : first + TILE, col : col + CHUNK] = head_norm(x)
            elif part == 1:
                keys[at, col : col + CHUNK] = head_norm(x)
            else:
                store_values(vext, at, col, x.astype(BF16))

        return begin, end

    def project_cross(first):
        def begin():
            return dot(hidden[first : first + TILE, :], wcq[...])

        def end(x):
            cq[first : first + TILE, :] = head_norm(x)

        return begin, end

    items = []
    for start in range(0, 3 * qwidth, CHUNK):
        tiles = [project(hidden, first, own, start) for first in range(0, rows, TILE)]
        if start >= qwidth:
            tiles += [project(near, first, other, start) for first in range(0, halo, TILE)]
        items += tiles
    items += [project_cross(first) for first in range(0, rows, TILE)]
    items.append(token_item(tokens, 0, wckv, ck, cvext))
    staggered(items)
    for copy in scalars:
        copy.wait()

    def self_item(pair, f, shifted):
        heads = [2 * pair, 2 * pair + 1]
        lanes = lanes_of(pair)
        inner = min(WMAX, blocks - 1 - f)
        count = WMAX + 1 + inner
        start = pl.multiple_of(local_block(f, odd, blocks) * BLK, BLK)
        first = pl.multiple_of(jnp.where(odd, f, blocks - 1 - f - inner) * BLK, BLK)
        at = pl.ds(first, count * BLK)

        def begin():
            return pair_scores(q[pl.ds(start, BLK), lanes], keys[at, lanes])

        def end(scores):
            bias = [[] for _ in heads]
            for mine_bias, h in zip(bias, heads):
                by_distance = [0.0] + [band_bias(band[h], d) for d in range(1, WMAX + 1)]
                for t in range(count):
                    one, two = abs(t - WMAX), abs(t - inner)
                    if one == two:
                        mine_bias.append(None if one == 0 else by_distance[one])
                    else:
                        mine_bias.append(jnp.where(odd, by_distance[one], by_distance[two]))
            scales = [factor[h] * (HD**-0.5 * LOG2E) for h in heads]
            part, weight, shifts = pair_sums(scores, vext[pair, at, :], scales, bias, shifted)
            if f < done:
                mine[f * BLK : (f + 1) * BLK, lanes] = (part / weight).astype(BF16)
                return
            to = slice((f - done) * BLK, (f - done + 1) * BLK)
            acc_out[to, lanes] = part
            sum_out[to, lanes] = weight
            if shifted:
                lane = lax.broadcasted_iota(jnp.int32, (BLK, LANES), 1)
                peaks = peak_out[to, :]
                for h, shift in zip(heads, shifts):
                    peaks = jnp.where(lane == h, shift, peaks)
                peak_out[to, :] = peaks

        return begin, end

    biases = [
        token_bias(
            align,
            counts,
            local_block(f, odd, blocks),
            device * (context.shape[0] // TOKB) - RCH,
            tokens.shape[0],
        )
        for f in range(done)
    ]

    def cross_item(pair, f, shifted):
        lanes = lanes_of(pair)
        start = pl.multiple_of(local_block(f, odd, blocks) * BLK, BLK)

        def begin():
            return pair_scores(cq[pl.ds(start, BLK), lanes], ck[:, lanes])

        def end(scores):
            scales = [temp[2 * pair + i] * (HD**-0.5 * LOG2E) for i in range(2)]
            part, weight, _ = pair_sums(
                scores, cvext[pair], scales, [[biases[f]]] * 2, shifted
            )
            cross_mine[f * BLK : (f + 1) * BLK, lanes] = (part / weight).astype(BF16)

        return begin, end

    pairs, cross_pairs = qwidth // LANES, cwidth // LANES
    easy = plain(factor, temp)

    def project_out():
        for load in loads:
            load.wait()
        total = dot(mine[...], wo[...]) + dot(cross_mine[...], wco[...])
        return finish(total, out, stage, sems, 0, done, odd, blocks)

    @pl.when(easy)
    def _():
        items = [cross_item(p, f, False) for p in range(cross_pairs) for f in range(done)]
        items += [self_item(p, f, False) for p in range(pairs) for f in range(done)]
        later = [self_item(p, f, False) for p in range(pairs) for f in range(done, blocks)]
        copies = []
        items += later[:2] + [(project_out, copies.extend)] + later[2:]
        staggered(items, 2)
        for copy in copies:
            copy.wait()

    @pl.when(jnp.logical_not(easy))
    def _():
        peak_out[...] = jnp.zeros_like(peak_out)

        @pl.loop(0, pairs)
        def _(p):
            staggered([self_item(p, f, True) for f in range(blocks)])

        @pl.loop(0, cross_pairs)
        def _(p):
            staggered([cross_item(p, f, True) for f in range(done)])

        for copy in project_out():
            copy.wait()


def tail_kernel(
    band_in,
    factor_in,
    temp_in,
    align_in,
    counts_in,
    pack,
    wqkv,
    wo,
    wco,
    wckv,
    ck_in,
    cvext_in,
    acc_in,
    sum_in,
    peak_in,
    q,
    cq,
    partial_out,
    out,
    band,
    factor,
    temp,
    align,
    counts,
    late,
    keys,
    vext,
    ck,
    cvext,
    mine,
    cross_mine,
    stage,
    sems,
):
    device = lax.axis_index("seq")
    odd = lax.rem(device, 2) == 1
    last = lax.axis_size("seq") - 1
    exists = jnp.where(odd, device < last, device > 0)
    rows, qwidth = q.shape
    blocks = rows // BLK
    halo = WMAX * BLK
    done = blocks - WMAX
    window, cwidth = ck.shape
    tokens = window - 2 * RCH * TOKB

    scalars = scalar_copies(
        (band_in, factor_in, temp_in, align_in, counts_in),
        (band, factor, temp, align, counts),
        sems,
        0,
    )
    vext[:, :, LANES:] = jnp.ones((vext.shape[0], vext.shape[1], LANES), BF16)
    ck[...] = ck_in[...]
    cvext[...] = cvext_in[...]
    late[...] = unpack_tokens(pack, halo, wckv.shape[0])
    late_at = pl.multiple_of(jnp.where(odd, window - RCH * TOKB, 0), 16)

    def project(first, start):
        def begin():
            return dot(pack[first : first + TILE, :], wqkv[:, start : start + CHUNK])

        def end(x):
            part, col = divmod(start, qwidth)
            at = slice(first, first + TILE)
            if part == 1:
                keys[at, col : col + CHUNK] = head_norm(x)
            else:
                store_values(vext, at, col, x.astype(BF16))

        return begin, end

    items = [token_item(late, late_at, wckv, ck, cvext)]
    items += [
        project(first, start)
        for start in range(qwidth, 3 * qwidth, CHUNK)
        for first in range(0, halo, TILE)
    ]
    staggered(items)
    for copy in scalars:
        copy.wait()

    def self_item(pair, f, shifted):
        heads = [2 * pair, 2 * pair + 1]
        lanes = lanes_of(pair)
        inner = blocks - 1 - f
        count = WMAX - inner
        start = pl.multiple_of(local_block(f, odd, blocks) * BLK, BLK)
        first = pl.multiple_of(jnp.where(odd, 0, halo - count * BLK), BLK)
        at = pl.ds(first, count * BLK)

        def begin():
            return pair_scores(q[pl.ds(start, BLK), lanes], keys[at, lanes])

        def end(scores):
            bias = [[] for _ in heads]
            for mine_bias, h in zip(bias, heads):
                width = jnp.where(exists, band[h], 0)
                for t in range(count):
                    one, two = band_bias(width, inner + 1 + t), band_bias(width, inner + count - t)
                    mine_bias.append(jnp.where(odd, one, two))
            scales = [factor[h] * (HD**-0.5 * LOG2E) for h in heads]
            part, weight, shifts = pair_sums(scores, vext[pair, at, :], scales, bias, shifted)
            to = slice((f - done) * BLK, (f - done + 1) * BLK)
            had, had_weight = acc_in[to, lanes], sum_in[to, lanes]
            if shifted:
                low = low_half(BLK)
                lane = lax.broadcasted_iota(jnp.int32, (BLK, LANES), 1)
                olds = [
                    jnp.sum(jnp.where(lane == h, peak_in[to, :], 0.0), axis=1, keepdims=True)
                    for h in heads
                ]
                news = [jnp.maximum(a, b) for a, b in zip(olds, shifts)]
                keep = [jnp.exp2(a - n) for a, n in zip(olds, news)]
                add = [jnp.exp2(b - n) for b, n in zip(shifts, news)]
                keep = jnp.where(low, keep[0], keep[1])
                add = jnp.where(low, add[0], add[1])
                had, had_weight = had * keep, had_weight * keep
                part, weight = part * add, weight * add
            mine[to, lanes] = ((had + part) / (had_weight + weight)).astype(BF16)

        return begin, end

    biases = [
        token_bias(
            align,
            counts,
            local_block(f, odd, blocks),
            device * (tokens // TOKB) - RCH,
            window,
        )
        for f in range(done, blocks)
    ]

    def cross_item(pair, f, shifted):
        lanes = lanes_of(pair)
        start = pl.multiple_of(local_block(f, odd, blocks) * BLK, BLK)

        def begin():
            return pair_scores(cq[pl.ds(start, BLK), lanes], ck[:, lanes])

        def end(scores):
            scales = [temp[2 * pair + i] * (HD**-0.5 * LOG2E) for i in range(2)]
            part, weight, _ = pair_sums(
                scores, cvext[pair], scales, [[biases[f - done]]] * 2, shifted
            )
            to = slice((f - done) * BLK, (f - done + 1) * BLK)
            cross_mine[to, lanes] = (part / weight).astype(BF16)

        return begin, end

    pairs, cross_pairs = qwidth // LANES, cwidth // LANES
    easy = plain(factor, temp)

    @pl.when(easy)
    def _():
        items = [
            cross_item(p, f, False) for p in range(cross_pairs) for f in range(done, blocks)
        ]
        items += [self_item(p, f, False) for p in range(pairs) for f in range(done, blocks)]
        staggered(items, 3)

    @pl.when(jnp.logical_not(easy))
    def _():
        @pl.loop(0, pairs)
        def _(p):
            staggered([self_item(p, f, True) for f in range(done, blocks)])

        @pl.loop(0, cross_pairs)
        def _(p):
            staggered([cross_item(p, f, True) for f in range(done, blocks)])

    copies = []
    for start in range(0, wo.shape[1], CHUNK):
        cols = slice(start, start + CHUNK)
        total = dot(mine[...], wo[:, cols]) + dot(cross_mine[...], wco[:, cols])
        stage[:, cols] = total.astype(BF16)
        for i in range(WMAX):
            to = pl.multiple_of(local_block(done + i, odd, blocks) * BLK, BLK)
            copies.append(
                pltpu.make_async_copy(
                    stage.at[pl.ds(i * BLK, BLK), pl.ds(start, CHUNK)],
                    out.at[pl.ds(to, BLK), pl.ds(start, CHUNK)],
                    sems.at[len(copies)],
                )
            )
            copies[-1].start()
    for copy in copies:
        copy.wait()


def shards(
    frames,
    context,
    noise_level,
    alignment,
    counts,
    band_width,
    mod_table,
    qkv_weight,
    out_weight,
    cross_query_weight,
    cross_kv_weight,
    cross_out_weight,
    banded_attender_factor,
    cross_temp,
):
    rows, width = frames.shape
    blocks = rows // BLK
    halo = WMAX * BLK
    done = blocks - WMAX
    tokens, cwidth = context.shape
    qwidth = qkv_weight.shape[1] // 3
    cqwidth = cross_query_weight.shape[1]
    pairs, cross_pairs = qwidth // LANES, cqwidth // LANES
    window = tokens + 2 * RCH * TOKB
    devices = lax.axis_size("seq")
    vmem = pl.BlockSpec(memory_space=pltpu.VMEM)
    hbm = pl.BlockSpec(memory_space=pltpu.HBM)
    pack_rows = halo + TOK_PACK

    hidden, near, far, context = pl.pallas_call(
        hidden_kernel,
        out_shape=[
            jax.ShapeDtypeStruct((rows, width), BF16),
            jax.ShapeDtypeStruct((pack_rows, width), BF16),
            jax.ShapeDtypeStruct((pack_rows, width), BF16),
            jax.ShapeDtypeStruct(context.shape, BF16),
        ],
        in_specs=[hbm] * 4,
        out_specs=[vmem] * 4,
        scratch_shapes=[
            pltpu.SMEM(noise_level.shape, jnp.int32),
            pltpu.VMEM(mod_table.shape, F32),
            pltpu.VMEM((rows, width), BF16),
            pltpu.SemaphoreType.DMA((blocks + 4,)),
        ],
        compiler_params=pltpu.CompilerParams(vmem_limit_bytes=8 * 2**20),
        cost_estimate=pl.CostEstimate(flops=8 * 10**9, bytes_accessed=4 * 10**6, transcendentals=0),
        name="hidden_and_packs",
    )(*in_hbm(noise_level, frames, mod_table, context))

    same_chip = [(i, i ^ 1) for i in range(devices) if i ^ 1 < devices]
    across = [(i, i + 1) for i in range(1, devices - 1, 2)]
    across += [(b, a) for a, b in across]
    near_got = lax.ppermute(near, "seq", same_chip)
    far_got = lax.ppermute(far, "seq", across)

    open_rows = WMAX * BLK
    scalar_scratch = [
        pltpu.SMEM(band_width.shape, jnp.int32),
        pltpu.SMEM(banded_attender_factor.shape, F32),
        pltpu.SMEM(cross_temp.shape, F32),
        pltpu.SMEM(alignment.shape[::-1], jnp.int32),
        pltpu.SMEM(counts.shape, jnp.int32),
    ]
    scalars = in_hbm(band_width, banded_attender_factor, cross_temp, alignment.T, counts)
    loads = 2
    update, acc, weight, peaks, q, cq, wo, wco, ck, cvext = pl.pallas_call(
        main_kernel,
        out_shape=[
            jax.ShapeDtypeStruct((rows, width), BF16),
            jax.ShapeDtypeStruct((open_rows, qwidth), F32),
            jax.ShapeDtypeStruct((open_rows, qwidth), F32),
            jax.ShapeDtypeStruct((open_rows, LANES), F32),
            jax.ShapeDtypeStruct((rows, qwidth), BF16),
            jax.ShapeDtypeStruct((rows, cqwidth), BF16),
            jax.ShapeDtypeStruct(out_weight.shape, BF16),
            jax.ShapeDtypeStruct(cross_out_weight.shape, BF16),
            jax.ShapeDtypeStruct((window, cqwidth), BF16),
            jax.ShapeDtypeStruct((cross_pairs, window, 2 * LANES), BF16),
        ],
        in_specs=[hbm] * 5 + [vmem] * 6 + [hbm] * 2,
        out_specs=[hbm] + [vmem] * 9,
        scratch_shapes=scalar_scratch
        + [
            pltpu.VMEM((window, cwidth), BF16),
            pltpu.VMEM((rows + halo, qwidth), BF16),
            pltpu.VMEM((pairs, rows + halo, 2 * LANES), BF16),
            pltpu.VMEM((done * BLK, qwidth), BF16),
            pltpu.VMEM((done * BLK, cqwidth), BF16),
            pltpu.VMEM((done * BLK, width), BF16),
            pltpu.SemaphoreType.DMA((loads + 5,)),
        ],
        compiler_params=pltpu.CompilerParams(vmem_limit_bytes=MAIN_VMEM),
        cost_estimate=pl.CostEstimate(
            flops=12 * 10**9, bytes_accessed=20 * 10**6, transcendentals=5 * 10**6
        ),
        name="local_attention",
    )(
        *scalars,
        hidden,
        near_got,
        context,
        qkv_weight,
        cross_query_weight,
        cross_kv_weight,
        *in_hbm(out_weight, cross_out_weight),
    )

    return pl.pallas_call(
        tail_kernel,
        out_shape=jax.ShapeDtypeStruct((rows, width), BF16),
        in_specs=[hbm] * 5 + [vmem] * 12 + [hbm],
        out_specs=hbm,
        scratch_shapes=scalar_scratch
        + [
            pltpu.VMEM((RCH * TOKB, cwidth), BF16),
            pltpu.VMEM((halo, qwidth), BF16),
            pltpu.VMEM((pairs, halo, 2 * LANES), BF16),
            pltpu.VMEM((window, cqwidth), BF16),
            pltpu.VMEM((cross_pairs, window, 2 * LANES), BF16),
            pltpu.VMEM((open_rows, qwidth), BF16),
            pltpu.VMEM((open_rows, cqwidth), BF16),
            pltpu.VMEM((open_rows, width), BF16),
            pltpu.SemaphoreType.DMA((max(5, WMAX * width // CHUNK),)),
        ],
        input_output_aliases={17: 0},
        compiler_params=pltpu.CompilerParams(vmem_limit_bytes=TAIL_VMEM),
        cost_estimate=pl.CostEstimate(
            flops=5 * 10**9, bytes_accessed=12 * 10**6, transcendentals=10**6
        ),
        name="halo_attention",
    )(
        *scalars,
        far_got,
        qkv_weight,
        wo,
        wco,
        cross_kv_weight,
        ck,
        cvext,
        acc,
        weight,
        peaks,
        q,
        cq,
        update,
    )


def solution(mesh):
    placed = (
        P(("groups", "seq"), None),
        P(("groups", "seq"), None),
        P(("groups", "seq")),
        P(("groups", "seq"), None),
        P(("groups", "seq")),
        P(),
        P(),
        P(),
        P(),
        P(),
        P(),
        P(),
        P(),
        P(),
    )
    return jax.shard_map(
        shards, mesh=mesh, in_specs=placed, out_specs=P(("groups", "seq"), None), check_vma=False
    )
```
